128 devices in a mesh: island: 8 (over x, y_lo), shard: 16 (over z, y_hi, core).
Axes of the slice: x: 4, y: 4 (y_hi: 2, y_lo: 2; y = y_hi * 2 + y_lo), z: 4, core: 2. Of those that a mesh axis runs over, the one named last changes fastest.
Arguments:
- partials: bfloat16 [8, 16, 512, 8192], P('island', 'shard'), may hold values from -6 to 6
- error_buf: float32 [8, 512, 8192], P('island', 'shard'), may hold values from -200 to 200
- momentum: float32 [512, 8192], P('shard'), may hold values from -6 to 6
- params: float32 [512, 8192], P('shard'), may hold values from -6 to 6
- start_q: float32 [8192, 256], P('shard'), may hold values from -6 to 6
Outputs:
- params_full: bfloat16 [512, 8192], replicated
- new_params: float32 [512, 8192], P('shard')
- new_momentum: float32 [512, 8192], P('shard')
- new_error: float32 [8, 512, 8192], P('island', 'shard')
The draws below stay inside these ranges and needn't reach their ends.
All inputs are finite; a program needn't handle non-finite values.
Results may differ from the reference program's by a relative error of at most 0.017.
Values may be sent and summed in bfloat16 or wider, within the bound.
No kernel may reach another device: no remote copies, remote signals or barrier semaphores. Data moves between devices by JAX's collectives and lax.ppermute only.
A program may use at most 128 MiB of HBM per device.

```python
import jax
import jax.numpy as jnp
from jax import lax

D = 8192
RANK = 256
NS_ITERS = 5
ROWS = 512
N_ISLAND = 8
N_SHARD = 16


def row_scaled(key, top, values):
    row_pos = jnp.arange(ROWS, dtype=jnp.float32) / max(ROWS - 1, 1)
    scales = jnp.exp(jnp.log(top) * row_pos)
    return values * scales[None, :, None]


def draw_error_buf(key, part):
    key = jax.random.fold_in(key, 7)
    values = jax.random.truncated_normal(key, -5.0, 5.0, (N_ISLAND, ROWS, D), jnp.float32)
    return row_scaled(key, 12.0, values)


def raised(array, key, source, target, parts, factor):
    def block_of(dim):
        return (jnp.arange(array.shape[dim]) // (array.shape[dim] // parts)).reshape((-1,) + (1,) * (array.ndim - 1 - dim))

    one_side = jax.random.permutation(key, parts)[block_of(target)]
    far = (block_of(target) + parts // 2) % parts
    return jnp.where((block_of(source) == one_side) | (block_of(source) == far), factor * array, array)


def block_scale(stream_key, shape, split, least, high):
    loudness = 1.0
    for dim, blocks in split:
        draws = jax.random.uniform(jax.random.fold_in(jax.random.fold_in(stream_key, 6), dim), (blocks,), jnp.float32, least / len(split), high / len(split))
        loudness = loudness * jnp.repeat(jnp.exp(draws), shape[dim] // blocks).reshape((-1,) + (1,) * (len(shape) - 1 - dim))
    return loudness


def noise(rng, extent, width, bound, pieces=(), held_as=jnp.bfloat16):
    entries = width * jax.random.normal(rng, extent, jnp.float32)
    if pieces:
        entries = entries * block_scale(rng, extent, pieces, -0.22, 0.18)
    return jnp.clip(entries, -bound, bound).astype(held_as)


def noise_with(rng, extent, width, most, cuts, heavy, kind=jnp.bfloat16):
    drawn = width * jax.random.normal(rng, extent, jnp.float32)
    if cuts:
        drawn = drawn * block_scale(rng, extent, cuts, -0.22, 0.18)
    return jnp.clip(raised(drawn, jax.random.fold_in(rng, 3), *heavy), -most, most).astype(kind)


def setup_inputs(seed: int = 0) -> dict:
    keys = jax.random.split(jax.random.key(seed), 6)
    partials = noise_with(keys[0], (N_ISLAND, N_SHARD, ROWS, D), 1.0, 6.0, ((0, 8), (1, 16)), (1, 2, 16, 2.0))
    error_buf = draw_error_buf(jax.random.fold_in(keys[5], 71), 0)
    momentum = noise(keys[2], (ROWS, D), 1.0, 6.0, ((0, 16),), jnp.float32)
    params = noise(keys[3], (ROWS, D), 1.0, 6.0, ((0, 16),), jnp.float32)
    start_q = noise(keys[4], (D, RANK), 1.0, 6.0, ((0, 16),), jnp.float32)
    return {"partials": partials, "error_buf": error_buf, "momentum": momentum, "params": params, "start_q": start_q}


HIGH = lax.Precision.HIGHEST

def reference(partials, error_buf, momentum, params, start_q):

    def add_member(s, acc):
        piece = lax.dynamic_index_in_dim(partials, s, 1, keepdims=False)
        return acc + piece.astype(jnp.float32)
    grads = lax.fori_loop(0, N_SHARD, add_member, jnp.zeros((N_ISLAND, ROWS, D), jnp.float32))
    merged = grads + error_buf
    proj = jnp.einsum('ird,dk->rk', merged, start_q, precision=HIGH) / N_ISLAND
    total = jnp.sum(proj * proj)
    orth = proj * lax.rsqrt(total + 1e-06)
    for step in range(NS_ITERS):
        gram_mat = jnp.dot(orth.T, orth, precision=HIGH)
        orth = 1.5 * orth - 0.5 * jnp.dot(orth, gram_mat, precision=HIGH)
    qnew = jnp.einsum('ird,rk->dk', merged, orth, precision=HIGH) / N_ISLAND
    delta = jnp.dot(orth, qnew.T, precision=HIGH)
    new_error = merged - delta[None]
    new_momentum = 0.9 * momentum + delta
    new_params = params - 0.7 * (delta + 0.9 * new_momentum)
    return (new_params.astype(jnp.bfloat16), new_params, new_momentum, new_error)
```

```python
import jax
import jax.numpy as jnp
from jax import lax
from jax.experimental import pallas as pl
from jax.experimental.pallas import tpu as pltpu
from jax.sharding import Mesh
from jax.sharding import PartitionSpec as P

NS_ITERS = 5
F32 = jnp.float32
BF16 = jnp.bfloat16
ISLAND = ("x", "ylo")
ZY = ("z", "yhi")
SHARD = ("z", "yhi", "core")
CHIPS = ("x", "ylo", "z", "yhi")
SWAP = [(0, 1), (1, 0)]


def dot_nn(left, right):
    return jnp.dot(left, right, preferred_element_type=F32)


def dot_tn(left, right):
    return lax.dot_general(left, right, (((0,), (0,)), ((), ())), preferred_element_type=F32)


def dot_nt(left, right):
    return lax.dot_general(left, right, (((1,), (1,)), ((), ())), preferred_element_type=F32)


def orth_kernel(proj_ref, orth_ref):
    proj = proj_ref[...]
    orth = proj * lax.rsqrt(jnp.sum(proj * proj) + 1e-06)
    for _ in range(NS_ITERS):
        low = orth.astype(BF16)
        gram_mat = dot_tn(low, low).astype(BF16)
        orth = 1.5 * orth - 0.5 * dot_nn(low, gram_mat)
    orth_ref[...] = orth


def orthogonalize(proj):
    return pl.pallas_call(
        orth_kernel, out_shape=jax.ShapeDtypeStruct(proj.shape, F32)
    )(proj)


def swap_cores(value):
    return lax.ppermute(value, "core", SWAP)


def to_all_chips(value):
    return lax.all_to_all(
        jnp.broadcast_to(value[None], (64,) + value.shape), CHIPS, 0, 0, tiled=True
    )


def on_device(partials, error_buf, momentum, params, start_q):
    core = lax.axis_index("core")
    isl = lax.axis_index(ISLAND)
    shard = lax.axis_index(SHARD)

    own_q = lax.dynamic_slice(start_q, ((isl % 4) * 128, 0), (128, 256)).astype(BF16)
    q_cols = jnp.where(isl // 4 == core, own_q, swap_cores(own_q))

    parts = partials[0, 0].reshape(8, 2, 32, 8192)
    theirs = lax.dynamic_index_in_dim(parts, 1 - core, 1, keepdims=False)
    ours = lax.dynamic_index_in_dim(parts, core, 1, keepdims=False)
    pair = (ours.astype(F32) + swap_cores(theirs).astype(F32)).astype(BF16)
    pieces = lax.all_to_all(pair, ZY, 0, 0, tiled=True)
    merged = jnp.sum(pieces.astype(F32), 0) + error_buf[0]

    blocks = merged.astype(BF16).reshape(32, 8, 8, 128).transpose(2, 1, 0, 3).reshape(64, 32, 128)
    blocks = lax.all_to_all(blocks, CHIPS, 0, 0, tiled=True).reshape(8, 256, 128)
    half = (jnp.sum(blocks.astype(F32), 0) * 0.125).astype(BF16)
    other_half = swap_cores(half)

    before = (params - (0.7 * 0.9 * 0.9) * momentum).astype(BF16)
    before, half = lax.optimization_barrier((before, half))
    before_full = lax.all_gather(before, SHARD, axis=0, tiled=True)

    local_proj = dot_nn(half, q_cols).astype(BF16)
    local_proj = local_proj.reshape(32, 8, 2, 128).transpose(0, 2, 1, 3).reshape(64, 8, 128)
    terms = lax.all_to_all(local_proj, CHIPS, 0, 0, tiled=True)
    piece = jnp.sum(terms.astype(F32), 0).astype(BF16)
    proj_half = to_all_chips(piece).reshape(32, 2, 8, 128).transpose(0, 2, 1, 3).reshape(8, 32, 256)
    proj_other = swap_cores(proj_half)
    proj = jnp.where(
        core == 0,
        jnp.stack([proj_half, proj_other], 1),
        jnp.stack([proj_other, proj_half], 1),
    ).reshape(512, 256)
    orth = orthogonalize(proj.astype(F32))
    low_orth = orth.astype(BF16)

    half = half.reshape(8, 32, 128)
    other_half = other_half.reshape(8, 32, 128)
    mean = jnp.where(
        core == 0,
        jnp.stack([half, other_half], 1),
        jnp.stack([other_half, half], 1),
    ).reshape(512, 128)
    qnew_cols = dot_tn(mean, low_orth).astype(BF16)
    qnew_mine = lax.dynamic_slice(qnew_cols, (core * 64, 0), (64, 256))
    qnew_mine = to_all_chips(qnew_mine)
    qnew_other = swap_cores(qnew_mine)
    qnew = jnp.where(
        core == 0,
        jnp.stack([qnew_mine, qnew_other], 1),
        jnp.stack([qnew_other, qnew_mine], 1),
    )
    qnew = qnew.reshape(8, 8, 128, 256).transpose(1, 0, 2, 3).reshape(8192, 256)

    delta_full = dot_nt(low_orth, qnew)
    params_full = (before_full.astype(F32) - (0.7 * 1.9) * delta_full).astype(BF16)
    orth_rows = lax.dynamic_slice(low_orth, (shard * 32, 0), (32, 256))
    delta = dot_nt(orth_rows, qnew)
    new_error = merged - delta
    new_momentum = 0.9 * momentum + delta
    new_params = params - 0.7 * (delta + 0.9 * new_momentum)
    return (params_full, new_params, new_momentum, new_error[None])


def solution(mesh):
    fine = Mesh(mesh.devices.reshape(4, 2, 4, 2, 2), ("x", "ylo", "z", "yhi", "core"))
    in_specs = (
        P(ISLAND, SHARD, None, None),
        P(ISLAND, SHARD, None),
        P(SHARD, None),
        P(SHARD, None),
        P(SHARD, None),
    )
    out_specs = (P(), P(SHARD, None), P(SHARD, None), P(ISLAND, SHARD, None))
    return jax.shard_map(
        on_device, mesh=fine, in_specs=in_specs, out_specs=out_specs, check_vma=False
    )
```

```python
import functools

import jax
import jax.numpy as jnp
from jax import lax
from jax.experimental import pallas as pl
from jax.experimental.pallas import tpu as pltpu
from jax.sharding import Mesh
from jax.sharding import PartitionSpec as P

NS_ITERS = 5
F32 = jnp.float32
BF16 = jnp.bfloat16
ISLAND = ("x", "ylo")
ZY = ("z", "yhi")
SHARD = ("z", "yhi", "core")
SWAP = [(0, 1), (1, 0)]
CHIPS = ("x", "ylo", "z", "yhi")
WIDE = 4096
VMEM = 60 * 1024 * 1024


def dot_nn(left, right):
    return jnp.dot(left, right, preferred_element_type=F32)


def dot_tn(left, right):
    return lax.dot_general(left, right, (((0,), (0,)), ((), ())), preferred_element_type=F32)


def dot_nt(left, right):
    return lax.dot_general(left, right, (((1,), (1,)), ((), ())), preferred_element_type=F32)


def factor_kernel(own_ref, other_ref, out):
    def left_factor(ref):
        return jnp.concatenate([ref[0], ref[1]], 1).astype(F32)

    own, other = left_factor(own_ref), left_factor(other_ref)
    scale = lax.rsqrt(jnp.sum(own * own) + jnp.sum(other * other) + 1e-06)
    own, other = own * scale, other * scale
    for _ in range(NS_ITERS):
        low_own, low_other = own.astype(BF16), other.astype(BF16)
        gram_mat = (dot_tn(low_own, low_own) + dot_tn(low_other, low_other)).astype(BF16)
        own = 1.5 * own - 0.5 * dot_nn(low_own, gram_mat)
        other = 1.5 * other - 0.5 * dot_nn(low_other, gram_mat)
    low_own, low_other = own.astype(BF16), other.astype(BF16)
    qnew = dot_tn(own_ref[2], low_own) + dot_tn(other_ref[2], low_other)
    delta = dot_nt(low_own, qnew.astype(BF16))
    weights = (own_ref[3].astype(F32) - (0.7 * 1.9) * delta).astype(BF16)
    delta = delta.astype(BF16).reshape(8, 32, 128)

    @pl.loop(0, 8)
    def _(island):
        for chip in range(8):
            out[island * 8 + chip, :256] = weights
            out[island * 8 + chip, 256:] = delta[chip]


def factors(own, other):
    vmem = pl.BlockSpec(memory_space=pltpu.VMEM)
    return pl.pallas_call(
        factor_kernel,
        in_specs=[vmem, vmem],
        out_specs=vmem,
        out_shape=jax.ShapeDtypeStruct((64, 288, 128), BF16),
        compiler_params=pltpu.CompilerParams(vmem_limit_bytes=32 * 1024 * 1024),
    )(own, other)


def put_weights(moved, full):
    for n in range(8):
        full[:, 0, :, n * 128 : (n + 1) * 128] = moved[n, 0, :256].reshape(8, 32, 128)


def own_kernel(place, moved, merged, momentum, params, full, new_params, new_momentum, new_error):
    put_weights(moved, full)
    for n in range(8):
        cols = slice(n * 128, (n + 1) * 128)
        delta = moved[n, 0, 256:].astype(F32)
        new_error[:, cols] = merged[:, cols] - delta
        step = 0.9 * momentum[:, cols] + delta
        new_momentum[:, cols] = step
        new_params[:, cols] = params[:, cols] - 0.7 * (delta + 0.9 * step)


def other_kernel(place, moved, _, full):
    put_weights(moved, full)


MOVED_SPEC = pl.BlockSpec((8, 1, 288, 128), lambda g, _: (0, g, 0, 0))
FULL_SHAPE = jax.ShapeDtypeStruct((8, 2, 32, 8192), BF16)


def own_rows(place, moved, merged, momentum, params):
    rows = pl.BlockSpec((32, 1024), lambda g, _: (0, g))
    row_shape = jax.ShapeDtypeStruct((32, 8192), F32)
    return pl.pallas_call(
        own_kernel,
        grid_spec=pltpu.PrefetchScalarGridSpec(
            num_scalar_prefetch=1,
            grid=(8,),
            in_specs=[MOVED_SPEC, rows, rows, rows],
            out_specs=[
                pl.BlockSpec((8, 1, 32, 1024), lambda g, at: (0, at[0], 0, g)), rows, rows, rows,
            ],
        ),
        out_shape=[FULL_SHAPE, row_shape, row_shape, row_shape],
        compiler_params=pltpu.CompilerParams(vmem_limit_bytes=VMEM),
    )(place, moved.reshape(8, 8, 288, 128), merged, momentum, params)


def other_rows(place, moved, full):
    return pl.pallas_call(
        other_kernel,
        grid_spec=pltpu.PrefetchScalarGridSpec(
            num_scalar_prefetch=1,
            grid=(8,),
            in_specs=[MOVED_SPEC, pl.BlockSpec(memory_space=pl.ANY)],
            out_specs=pl.BlockSpec((8, 1, 32, 1024), lambda g, at: (0, 1 - at[0], 0, g)),
        ),
        out_shape=FULL_SHAPE,
        input_output_aliases={2: 0},
        compiler_params=pltpu.CompilerParams(vmem_limit_bytes=VMEM),
    )(place, moved.reshape(8, 8, 288, 128), full)


def swap_cores(value):
    return lax.ppermute(value, "core", SWAP)


def along_z(value, step):
    return lax.ppermute(value, "z", [(at, (at + step) % 4) for at in range(4)])


def copies(value, axes):
    count = lax.axis_size(axes)
    value = jnp.broadcast_to(value[None], (count,) + value.shape)
    return lax.all_to_all(value, axes, 0, 0, tiled=True)


def ring_order(ring, z):
    ring = jnp.stack([ring[0], ring[3], ring[2], ring[1]])
    return lax.dynamic_slice_in_dim(jnp.concatenate([ring, ring]), (4 - z) % 4, 4, 0)


def block_at(place, k, j, side):
    return lax.rem(place[1] + k, 4) * 4 + lax.rem(place[2] + j, 2) * 2 + lax.rem(place[0] + side, 2)


BLOCKS = [(k, j) for k in range(4) for j in range(2)]


def block_copies(place, parts, out, sems, side, half):
    return [
        pltpu.make_async_copy(
            parts.at[block_at(place, k, j, side), :, pl.ds(half * WIDE, WIDE)],
            out.at[k, j],
            sems.at[k, j],
        )
        for k, j in BLOCKS
    ]


def theirs_kernel(half, place, parts, out, sems):
    copies = block_copies(place, parts, out, sems, 1, half)
    for copy in copies:
        copy.start()
    for copy in copies:
        copy.wait()


def theirs(place, parts, half):
    return pl.pallas_call(
        functools.partial(theirs_kernel, half),
        in_specs=[
            pl.BlockSpec(memory_space=pltpu.SMEM),
            pl.BlockSpec(memory_space=pl.ANY),
        ],
        out_specs=pl.BlockSpec(memory_space=pltpu.VMEM),
        out_shape=pltpu.VMEM((4, 2, 32, WIDE), BF16),
        scratch_shapes=[pltpu.SemaphoreType.DMA((4, 2))],
    )(place, parts)


def add(left, right):
    return (left.astype(F32) + right.astype(F32)).astype(BF16)


def pair_sums(half, place, parts, received, ours, theirs, sems, in_sems):
    copies = list(zip(
        block_copies(place, parts, ours, sems, 0, half),
        [pltpu.make_async_copy(received.at[k, j], theirs.at[k, j], in_sems.at[k, j]) for k, j in BLOCKS],
    ))
    for own, other in copies:
        own.start()
        other.start()
    for (k, j), (own, other) in zip(BLOCKS, copies):
        own.wait()
        other.wait()
        yield k, j, add(ours[k, j], theirs[k, j])


def right_kernel(place, parts, received, keep, send, *scratch):
    for k, j, total in pair_sums(1, place, parts, received, *scratch):
        (send if j else keep)[k] = total


def left_kernel(place, parts, received, piece, keep, up, far, down, *scratch):
    outs = (keep, up, far, down)
    for out in outs[1:]:
        out[:, WIDE:] = piece[...]
    for k, j, total in pair_sums(0, place, parts, received, *scratch):
        outs[k][32 * j : 32 * j + 32, :WIDE] = total


def pair_call(kernel, shapes, place, parts, received, *rest):
    vmem = pl.BlockSpec(memory_space=pltpu.VMEM)
    anywhere = pl.BlockSpec(memory_space=pl.ANY)
    return pl.pallas_call(
        kernel,
        in_specs=[pl.BlockSpec(memory_space=pltpu.SMEM), anywhere, anywhere] + [vmem] * len(rest),
        out_specs=[vmem] * len(shapes),
        out_shape=[pltpu.VMEM(shape, BF16) for shape in shapes],
        scratch_shapes=[pltpu.VMEM((4, 2, 32, WIDE), BF16)] * 2 + [pltpu.SemaphoreType.DMA((4, 2))] * 2,
    )(place, parts, received, *rest)


def turn_kernel(left, up, far, down, piece, keep, back):
    def total(rows):
        value = left[rows, :].astype(F32)
        for ref in (up, far, down):
            value = value + ref[rows, :WIDE].astype(F32)
        return value

    keep[...] = total(slice(0, 32))
    back[:, :WIDE] = total(slice(32, 64)).astype(BF16)
    for k, ref in enumerate((piece, up, far, down)):
        at = 0 if k == 0 else WIDE
        for j in range(2):
            back[:, WIDE + k * 1024 + j * 512 : WIDE + k * 1024 + (j + 1) * 512] = ref[
                32 * j : 32 * j + 32, at : at + 512
            ]


def turn(left, up, far, down, piece):
    vmem = pl.BlockSpec(memory_space=pltpu.VMEM)
    return pl.pallas_call(
        turn_kernel,
        in_specs=[vmem] * 5,
        out_specs=[vmem] * 2,
        out_shape=[pltpu.VMEM((32, WIDE), F32), pltpu.VMEM((32, 2 * WIDE), BF16)],
    )(left, up, far, down, piece)


def summed_rows(partials, piece, place, z, yhi):
    parts = partials.reshape(16, 32, 8192)
    right_out, parts_later = lax.optimization_barrier((theirs(place, parts, 1), parts))
    right_in, left_in = swap_cores(right_out), swap_cores(theirs(place, parts_later, 0))
    right, across = pair_call(right_kernel, [(4, 32, WIDE)] * 2, place, parts, right_in)
    left_in, right = lax.optimization_barrier((left_in, right))
    across = lax.ppermute(across, "yhi", SWAP)
    shapes = [(64, WIDE)] + [(64, WIDE + 512)] * 3
    left, up, far, down = pair_call(left_kernel, shapes, place, parts, left_in, piece)
    far, up, down = along_z(far, 2), along_z(up, 1), along_z(down, 3)
    sums = [right[k].astype(F32) + across[k].astype(F32) for k in range(4)]
    moved = [along_z(sums[k].astype(BF16), k) for k in (2, 1, 3)]
    left, sent = turn(left, up, far, down, piece)
    back = lax.ppermute(sent, "yhi", SWAP)
    right = sums[0] + sum(moved_in.astype(F32) for moved_in in moved)
    left = left + back[:, :WIDE].astype(F32)
    ours, others = (
        ring_order([value[:, WIDE + k * 1024 : WIDE + (k + 1) * 1024] for k in range(4)], z)
        for value in (sent, back)
    )
    pieces = jnp.where(yhi == 0, jnp.stack([ours, others], 1), jnp.stack([others, ours], 1))
    return jnp.concatenate([left, right], 1), pieces.reshape(8, 32, 4, 256)


def on_device(partials, error_buf, momentum, params, start_q):
    core, z, yhi = (lax.axis_index(name) for name in ("core", "z", "yhi"))
    isl = lax.axis_index(ISLAND)
    place = jnp.stack([core, z, yhi]).astype(jnp.int32)

    own_q = lax.dynamic_slice(start_q, ((isl % 4) * 128, 0), (128, 256)).astype(BF16)
    piece = jnp.concatenate([own_q[:64], own_q[64:]], 1)
    merged, pieces = summed_rows(partials[0, 0], piece, place, z, yhi)
    merged = merged + error_buf[0]
    q_own = jnp.stack([pieces[:, :, n] for n in (0, 2, 1, 3)], 1).reshape(1024, 256)
    q_cols = jnp.where(isl // 4 == core, q_own, swap_cores(q_own))

    def columns(value):
        return lax.dynamic_index_in_dim(value.reshape(32, 8, 8, 128), isl, 2, False)

    before = (columns(params) - (0.7 * 0.9 * 0.9) * columns(momentum)).astype(BF16)
    before = before.transpose(1, 0, 2)

    blocks = merged.astype(BF16).reshape(32, 8, 8, 128).transpose(2, 1, 0, 3)
    blocks = lax.all_to_all(blocks, ISLAND, 0, 0, tiled=True)
    mean = (jnp.sum(blocks.astype(F32), 0) * 0.125).astype(BF16)
    local_proj = dot_nn(mean.transpose(1, 0, 2).reshape(32, 1024), q_cols).astype(BF16)
    proj = jnp.sum(copies(local_proj, ISLAND).astype(F32), 0).astype(BF16)

    proj = proj.reshape(32, 2, 128).transpose(1, 0, 2)
    proj = jnp.broadcast_to(proj[None], (8, 2, 32, 128))
    own = jnp.concatenate([proj, mean[:, None], before[:, None]], 1)
    own = lax.all_to_all(own, ZY, 0, 0, tiled=True).transpose(1, 0, 2, 3).reshape(4, 256, 128)
    other = swap_cores(own)

    moved_own = lax.all_to_all(factors(own, other), CHIPS, 0, 0, tiled=True)
    moved_other = swap_cores(moved_own)
    params_full, new_params, new_momentum, new_error = own_rows(
        place, moved_own, merged, momentum, params
    )
    params_full = other_rows(place, moved_other, params_full)
    return (params_full.reshape(512, 8192), new_params, new_momentum, new_error[None])


def solution(mesh):
    fine = Mesh(mesh.devices.reshape(4, 2, 4, 2, 2), ("x", "ylo", "z", "yhi", "core"))
    in_specs = (
        P(ISLAND, SHARD, None, None),
        P(ISLAND, SHARD, None),
        P(SHARD, None),
        P(SHARD, None),
        P(SHARD, None),
    )
    out_specs = (P(), P(SHARD, None), P(SHARD, None), P(ISLAND, SHARD, None))
    return jax.shard_map(
        on_device, mesh=fine, in_specs=in_specs, out_specs=out_specs, check_vma=False
    )
```

```python
import functools

import jax
import jax.numpy as jnp
from jax import lax
from jax.experimental import pallas as pl
from jax.experimental.pallas import tpu as pltpu
from jax.sharding import Mesh
from jax.sharding import PartitionSpec as P

NS_ITERS = 5
F32 = jnp.float32
BF16 = jnp.bfloat16
ISLAND = ("x", "ylo")
ZY = ("z", "yhi")
SHARD = ("z", "yhi", "core")
SWAP = [(0, 1), (1, 0)]
CHIPS = ("x", "ylo", "z", "yhi")
WIDE = 4096
VMEM = 60 * 1024 * 1024


def dot_nn(left, right):
    return jnp.dot(left, right, preferred_element_type=F32)


def dot_tn(left, right):
    return lax.dot_general(left, right, (((0,), (0,)), ((), ())), preferred_element_type=F32)


def dot_nt(left, right):
    return lax.dot_general(left, right, (((1,), (1,)), ((), ())), preferred_element_type=F32)


def factor_kernel(own_ref, other_ref, out):
    def left_factor(ref):
        return jnp.concatenate([ref[0], ref[1]], 1).astype(F32)

    own, other = left_factor(own_ref), left_factor(other_ref)
    scale = lax.rsqrt(jnp.sum(own * own) + jnp.sum(other * other) + 1e-06)
    own, other = own * scale, other * scale
    for _ in range(NS_ITERS):
        low_own, low_other = own.astype(BF16), other.astype(BF16)
        gram_mat = (dot_tn(low_own, low_own) + dot_tn(low_other, low_other)).astype(BF16)
        own = 1.5 * own - 0.5 * dot_nn(low_own, gram_mat)
        other = 1.5 * other - 0.5 * dot_nn(low_other, gram_mat)
    low_own, low_other = own.astype(BF16), other.astype(BF16)
    qnew = dot_tn(own_ref[2], low_own) + dot_tn(other_ref[2], low_other)
    delta = dot_nt(low_own, qnew.astype(BF16))
    weights = (own_ref[3].astype(F32) - (0.7 * 1.9) * delta).astype(BF16)
    delta = delta.astype(BF16).reshape(8, 32, 128)

    @pl.loop(0, 8)
    def _(island):
        for chip in range(8):
            out[island * 8 + chip, :256] = weights
            out[island * 8 + chip, 256:] = delta[chip]


def factors(own, other):
    vmem = pl.BlockSpec(memory_space=pltpu.VMEM)
    return pl.pallas_call(
        factor_kernel,
        in_specs=[vmem, vmem],
        out_specs=vmem,
        out_shape=jax.ShapeDtypeStruct((64, 288, 128), BF16),
        compiler_params=pltpu.CompilerParams(vmem_limit_bytes=32 * 1024 * 1024),
    )(own, other)


def block_cols(g):
    return pl.ds(g * 1024, 1024)


def put_weights(moved, full):
    for n in range(8):
        full[:, :, n * 128 : (n + 1) * 128] = moved[n, :256].reshape(8, 32, 128)


def own_kernel(place, *refs):
    ins, outs, rest = refs[:4], refs[4:8], refs[8:]
    held, made, in_sems, out_sems = rest[:4], rest[4:8], rest[8], rest[9]
    loads, stores = [], []
    for g in range(8):
        views = [ins[0].at[:, g]] + [ref.at[:, block_cols(g)] for ref in ins[1:]]
        loads.append([
            pltpu.make_async_copy(view, to.at[g], in_sems.at[n, g])
            for n, (view, to) in enumerate(zip(views, held))
        ])
        views = [outs[0].at[:, place[0], :, block_cols(g)]]
        views += [ref.at[:, block_cols(g)] for ref in outs[1:]]
        stores.append([
            pltpu.make_async_copy(of.at[g], view, out_sems.at[n, g])
            for n, (of, view) in enumerate(zip(made, views))
        ])
    for copies in loads:
        for copy in copies:
            copy.start()
    moved, merged, momentum, params = held
    full, new_params, new_momentum, new_error = made
    for g in range(8):
        for copy in loads[g]:
            copy.wait()
        put_weights(moved.at[g], full.at[g])
        for n in range(8):
            at = (g, slice(None), slice(n * 128, (n + 1) * 128))
            delta = moved[g, n, 256:].astype(F32)
            new_error[at] = merged[at] - delta
            step = 0.9 * momentum[at] + delta
            new_momentum[at] = step
            new_params[at] = params[at] - 0.7 * (delta + 0.9 * step)
        for copy in stores[g]:
            copy.start()
    for copies in stores:
        for copy in copies:
            copy.wait()


FULL_SHAPE = jax.ShapeDtypeStruct((8, 2, 32, 8192), BF16)
SMEM = pl.BlockSpec(memory_space=pltpu.SMEM)
ANYWHERE = pl.BlockSpec(memory_space=pl.ANY)


def own_rows(place, moved, merged, momentum, params):
    row_shape = jax.ShapeDtypeStruct((32, 8192), F32)
    rows = pltpu.VMEM((8, 32, 1024), F32)
    return pl.pallas_call(
        own_kernel,
        in_specs=[SMEM] + [ANYWHERE] * 4,
        out_specs=[ANYWHERE] * 4,
        out_shape=[FULL_SHAPE, row_shape, row_shape, row_shape],
        scratch_shapes=[
            pltpu.VMEM((8, 8, 288, 128), BF16), rows, rows, rows,
            pltpu.VMEM((8, 8, 32, 1024), BF16), rows, rows, rows,
            pltpu.SemaphoreType.DMA((4, 8)),
            pltpu.SemaphoreType.DMA((4, 8)),
        ],
        compiler_params=pltpu.CompilerParams(vmem_limit_bytes=VMEM),
    )(place, moved.reshape(8, 8, 288, 128), merged, momentum, params)


def other_kernel(place, moved, _, full, held, made, in_sems, out_sems):
    side = 1 - place[0]
    loads = [
        pltpu.make_async_copy(moved.at[:, g, pl.ds(0, 256)], held.at[g], in_sems.at[g])
        for g in range(8)
    ]
    stores = [
        pltpu.make_async_copy(made.at[g], full.at[:, side, :, block_cols(g)], out_sems.at[g])
        for g in range(8)
    ]
    for copy in loads:
        copy.start()
    for g in range(8):
        loads[g].wait()
        put_weights(held.at[g], made.at[g])
        stores[g].start()
    for copy in stores:
        copy.wait()


def other_rows(place, moved, full):
    return pl.pallas_call(
        other_kernel,
        in_specs=[SMEM, ANYWHERE, ANYWHERE],
        out_specs=ANYWHERE,
        out_shape=FULL_SHAPE,
        input_output_aliases={2: 0},
        scratch_shapes=[
            pltpu.VMEM((8, 8, 256, 128), BF16),
            pltpu.VMEM((8, 8, 32, 1024), BF16),
            pltpu.SemaphoreType.DMA((8,)),
            pltpu.SemaphoreType.DMA((8,)),
        ],
        compiler_params=pltpu.CompilerParams(vmem_limit_bytes=VMEM),
    )(place, moved.reshape(8, 8, 288, 128), full)


def middle_kernel(place, blocks, q_own, q_other, mean, out):
    total = blocks[0].astype(F32)
    for n in range(1, 8):
        total = total + blocks[n].astype(F32)
    low = (total * 0.125).astype(BF16)
    mean[...] = low
    low = jnp.concatenate([low[n] for n in range(8)], 1)
    for flag, q_ref in ((1, q_own), (0, q_other)):

        @pl.when(place[3] == flag)
        def _():
            value = dot_nn(low, q_ref[...]).astype(BF16)
            for n in range(8):
                out[n] = value


def middle(place, blocks, q_own, q_other):
    vmem = pl.BlockSpec(memory_space=pltpu.VMEM)
    return pl.pallas_call(
        middle_kernel,
        in_specs=[SMEM] + [vmem] * 3,
        out_specs=[vmem] * 2,
        out_shape=[
            pltpu.VMEM((8, 32, 128), BF16),
            jax.ShapeDtypeStruct((8, 32, 256), BF16),
        ],
    )(place, blocks, q_own, q_other)


def gather_kernel(terms, mean, before, out):
    total = terms[0].astype(F32)
    for n in range(1, 8):
        total = total + terms[n].astype(F32)
    total = total.astype(BF16)
    for n in range(8):
        out[n, 0] = total[:, :128]
        out[n, 1] = total[:, 128:]
        out[n, 2] = mean[n]
        out[n, 3] = before[n]


def gathered(terms, mean, before):
    vmem = pl.BlockSpec(memory_space=pltpu.VMEM)
    return pl.pallas_call(
        gather_kernel,
        in_specs=[vmem] * 3,
        out_specs=vmem,
        out_shape=jax.ShapeDtypeStruct((8, 4, 32, 128), BF16),
    )(terms, mean, before)


def merge_kernel(left, back, right, far, up, down, error, merged, blocks):
    for n in range(64):
        at = slice((n % 32) * 128, (n % 32 + 1) * 128)
        if n < 32:
            value = left[:, at] + back[:, at].astype(F32)
        else:
            value = right[:, at]
            for ref in (far, up, down):
                value = value + ref[:, at].astype(F32)
        value = value + error[:, n * 128 : (n + 1) * 128]
        merged[:, n * 128 : (n + 1) * 128] = value
        blocks[n % 8, n // 8] = value.astype(BF16)


def merge(left, back, right, moved, error):
    vmem = pl.BlockSpec(memory_space=pltpu.VMEM)
    return pl.pallas_call(
        merge_kernel,
        in_specs=[vmem] * 7,
        out_specs=[vmem] * 2,
        out_shape=[
            jax.ShapeDtypeStruct((32, 8192), F32),
            jax.ShapeDtypeStruct((8, 8, 32, 128), BF16),
        ],
    )(left, back, right, *moved, error)


def swap_cores(value):
    return lax.ppermute(value, "core", SWAP)


def along_z(value, step):
    return lax.ppermute(value, "z", [(at, (at + step) % 4) for at in range(4)])


def ring_order(ring, z):
    ring = jnp.stack([ring[0], ring[3], ring[2], ring[1]])
    return lax.dynamic_slice_in_dim(jnp.concatenate([ring, ring]), (4 - z) % 4, 4, 0)


def block_at(place, k, j, side):
    return lax.rem(place[1] + k, 4) * 4 + lax.rem(place[2] + j, 2) * 2 + lax.rem(place[0] + side, 2)


BLOCKS = [(k, j) for k in range(4) for j in range(2)]


def block_copies(place, parts, out, sems, side, half):
    return [
        pltpu.make_async_copy(
            parts.at[block_at(place, k, j, side), :, pl.ds(half * WIDE, WIDE)],
            out.at[k, j],
            sems.at[k, j],
        )
        for k, j in BLOCKS
    ]


def theirs_kernel(half, place, parts, out, sems):
    copies = block_copies(place, parts, out, sems, 1, half)
    for copy in copies:
        copy.start()
    for copy in copies:
        copy.wait()


def theirs(place, parts, half):
    return pl.pallas_call(
        functools.partial(theirs_kernel, half),
        in_specs=[
            pl.BlockSpec(memory_space=pltpu.SMEM),
            pl.BlockSpec(memory_space=pl.ANY),
        ],
        out_specs=pl.BlockSpec(memory_space=pltpu.VMEM),
        out_shape=pltpu.VMEM((4, 2, 32, WIDE), BF16),
        scratch_shapes=[pltpu.SemaphoreType.DMA((4, 2))],
    )(place, parts)


def add(left, right):
    return (left.astype(F32) + right.astype(F32)).astype(BF16)


def pair_sums(half, place, parts, received, ours, theirs, sems, in_sems):
    copies = list(zip(
        block_copies(place, parts, ours, sems, 0, half),
        [pltpu.make_async_copy(received.at[k, j], theirs.at[k, j], in_sems.at[k, j]) for k, j in BLOCKS],
    ))
    for own, other in copies:
        own.start()
        other.start()
    for (k, j), (own, other) in zip(BLOCKS, copies):
        own.wait()
        other.wait()
        yield k, j, add(ours[k, j], theirs[k, j])


def right_kernel(place, parts, received, keep, send, *scratch):
    for k, j, total in pair_sums(1, place, parts, received, *scratch):
        (send if j else keep)[k] = total


def left_kernel(place, parts, received, piece, keep, up, far, down, *scratch):
    outs = (keep, up, far, down)
    for out in outs[1:]:
        out[:, WIDE:] = piece[...]
    for k, j, total in pair_sums(0, place, parts, received, *scratch):
        outs[k][32 * j : 32 * j + 32, :WIDE] = total


def pair_call(kernel, shapes, place, parts, received, *rest):
    vmem = pl.BlockSpec(memory_space=pltpu.VMEM)
    anywhere = pl.BlockSpec(memory_space=pl.ANY)
    return pl.pallas_call(
        kernel,
        in_specs=[pl.BlockSpec(memory_space=pltpu.SMEM), anywhere, anywhere] + [vmem] * len(rest),
        out_specs=[vmem] * len(shapes),
        out_shape=[pltpu.VMEM(shape, BF16) for shape in shapes],
        scratch_shapes=[pltpu.VMEM((4, 2, 32, WIDE), BF16)] * 2 + [pltpu.SemaphoreType.DMA((4, 2))] * 2,
    )(place, parts, received, *rest)


def turn_kernel(left, up, far, down, piece, keep, back):
    def total(rows):
        value = left[rows, :].astype(F32)
        for ref in (up, far, down):
            value = value + ref[rows, :WIDE].astype(F32)
        return value

    keep[...] = total(slice(0, 32))
    back[:, :WIDE] = total(slice(32, 64)).astype(BF16)
    for k, ref in enumerate((piece, up, far, down)):
        at = 0 if k == 0 else WIDE
        for j in range(2):
            back[:, WIDE + k * 1024 + j * 512 : WIDE + k * 1024 + (j + 1) * 512] = ref[
                32 * j : 32 * j + 32, at : at + 512
            ]


def turn(left, up, far, down, piece):
    vmem = pl.BlockSpec(memory_space=pltpu.VMEM)
    return pl.pallas_call(
        turn_kernel,
        in_specs=[vmem] * 5,
        out_specs=[vmem] * 2,
        out_shape=[pltpu.VMEM((32, WIDE), F32), pltpu.VMEM((32, 2 * WIDE), BF16)],
    )(left, up, far, down, piece)


def summed_rows(partials, error, piece, place, z, yhi):
    parts = partials.reshape(16, 32, 8192)
    left_out, parts_later = lax.optimization_barrier((theirs(place, parts, 0), parts))
    left_in, right_in = swap_cores(left_out), swap_cores(theirs(place, parts_later, 1))
    shapes = [(64, WIDE)] + [(64, WIDE + 512)] * 3
    left, up, far, down = pair_call(left_kernel, shapes, place, parts, left_in, piece)
    right_in, left = lax.optimization_barrier((right_in, left))
    right, across = pair_call(right_kernel, [(4, 32, WIDE)] * 2, place, parts, right_in)
    across = lax.ppermute(across, "yhi", SWAP)
    far, up, down = along_z(far, 2), along_z(up, 1), along_z(down, 3)
    sums = [right[k].astype(F32) + across[k].astype(F32) for k in range(4)]
    moved = [along_z(sums[k].astype(BF16), k) for k in (2, 1, 3)]
    left, sent = turn(left, up, far, down, piece)
    back = lax.ppermute(sent, "yhi", SWAP)
    merged, blocks = merge(left, back, sums[0], moved, error)
    ours, others = (
        ring_order([value[:, WIDE + k * 1024 : WIDE + (k + 1) * 1024] for k in range(4)], z)
        for value in (sent, back)
    )
    pieces = jnp.where(yhi == 0, jnp.stack([ours, others], 1), jnp.stack([others, ours], 1))
    return merged, blocks, pieces.reshape(8, 32, 4, 256)


def on_device(partials, error_buf, momentum, params, start_q):
    core, z, yhi = (lax.axis_index(name) for name in ("core", "z", "yhi"))
    isl = lax.axis_index(ISLAND)
    place = jnp.stack([core, z, yhi, isl // 4 == core]).astype(jnp.int32)

    own_q = lax.dynamic_slice(start_q, ((isl % 4) * 128, 0), (128, 256)).astype(BF16)
    piece = jnp.concatenate([own_q[:64], own_q[64:]], 1)
    merged, blocks, pieces = summed_rows(partials[0, 0], error_buf[0], piece, place, z, yhi)
    q_own = jnp.stack([pieces[:, :, n] for n in (0, 2, 1, 3)], 1).reshape(1024, 256)
    q_other = swap_cores(q_own)

    def columns(value):
        return lax.dynamic_index_in_dim(value.reshape(32, 8, 8, 128), isl, 2, False)

    before = (columns(params) - (0.7 * 0.9 * 0.9) * columns(momentum)).astype(BF16)
    before = before.transpose(1, 0, 2)

    blocks = lax.all_to_all(blocks, ISLAND, 0, 0, tiled=True)
    mean, terms = middle(place, blocks, q_own, q_other)
    terms = lax.all_to_all(terms, ISLAND, 0, 0, tiled=True)

    own = lax.all_to_all(gathered(terms, mean, before), ZY, 0, 0, tiled=True)
    own = own.transpose(1, 0, 2, 3).reshape(4, 256, 128)
    other = swap_cores(own)

    moved_own = lax.all_to_all(factors(own, other), CHIPS, 0, 0, tiled=True)
    moved_other = swap_cores(moved_own)
    params_full, new_params, new_momentum, new_error = own_rows(
        place, moved_own, merged, momentum, params
    )
    params_full = other_rows(place, moved_other, params_full)
    return (params_full.reshape(512, 8192), new_params, new_momentum, new_error[None])


def solution(mesh):
    fine = Mesh(mesh.devices.reshape(4, 2, 4, 2, 2), ("x", "ylo", "z", "yhi", "core"))
    in_specs = (
        P(ISLAND, SHARD, None, None),
        P(ISLAND, SHARD, None),
        P(SHARD, None),
        P(SHARD, None),
        P(SHARD, None),
    )
    out_specs = (P(), P(SHARD, None), P(SHARD, None), P(ISLAND, SHARD, None))
    return jax.shard_map(
        on_device, mesh=fine, in_specs=in_specs, out_specs=out_specs, check_vma=False
    )
```

```python
import functools

import jax
import jax.numpy as jnp
from jax import lax
from jax.experimental import pallas as pl
from jax.experimental.pallas import tpu as pltpu
from jax.sharding import Mesh
from jax.sharding import PartitionSpec as P

NS_ITERS = 5
F32 = jnp.float32
BF16 = jnp.bfloat16
ISLAND = ("x", "ylo")
ZY = ("z", "yhi")
SHARD = ("z", "yhi", "core")
SWAP = [(0, 1), (1, 0)]
CHIPS = ("x", "ylo", "z", "yhi")
WIDE = 4096
VMEM = 60 * 1024 * 1024


def dot_nn(left, right):
    return jnp.dot(left, right, preferred_element_type=F32)


def dot_tn(left, right):
    return lax.dot_general(left, right, (((0,), (0,)), ((), ())), preferred_element_type=F32)


def dot_nt(left, right):
    return lax.dot_general(left, right, (((1,), (1,)), ((), ())), preferred_element_type=F32)


def updated(before, delta):
    return (before.astype(F32) - (0.7 * 1.9) * delta.astype(F32)).astype(BF16)


def factor_kernel(own_ref, other_ref, out):
    def left_factor(ref):
        return jnp.concatenate([ref[0], ref[1]], 1).astype(F32)

    own, other = left_factor(own_ref), left_factor(other_ref)
    scale = lax.rsqrt(jnp.sum(own * own) + jnp.sum(other * other) + 1e-06)
    own, other = own * scale, other * scale
    for _ in range(NS_ITERS):
        low_own, low_other = own.astype(BF16), other.astype(BF16)
        gram_mat = (dot_tn(low_own, low_own) + dot_tn(low_other, low_other)).astype(BF16)
        own = 1.5 * own - 0.5 * dot_nn(low_own, gram_mat)
        other = 1.5 * other - 0.5 * dot_nn(low_other, gram_mat)
    low_own, low_other = own.astype(BF16), other.astype(BF16)
    qnew = dot_tn(own_ref[2], low_own) + dot_tn(other_ref[2], low_other)
    delta = dot_nt(low_own, qnew.astype(BF16)).astype(BF16)
    weights = updated(own_ref[3], delta)
    delta = delta.reshape(8, 32, 128)

    @pl.loop(0, 8)
    def _(island):
        for chip in range(8):
            out[island * 8 + chip] = weights
            out[island * 8 + chip, chip * 32 : chip * 32 + 32] = delta[chip]


def factors(own, other):
    vmem = pl.BlockSpec(memory_space=pltpu.VMEM)
    return pl.pallas_call(
        factor_kernel,
        in_specs=[vmem, vmem],
        out_specs=vmem,
        out_shape=jax.ShapeDtypeStruct((64, 256, 128), BF16),
        compiler_params=pltpu.CompilerParams(vmem_limit_bytes=32 * 1024 * 1024),
    )(own, other)


def block_cols(g):
    return pl.ds(g * 1024, 1024)


def put_weights(moved, before, full, chip):
    at = pl.ds(pl.multiple_of(chip * 32, 32), 32)
    deltas = []
    for n in range(8):
        cols = slice(n * 128, (n + 1) * 128)
        full[:, :, cols] = moved[n].reshape(8, 32, 128)
        deltas.append(moved[n, at, :])
        full[pl.ds(chip, 1), :, cols] = updated(before[:, cols], deltas[n])[None]
    return deltas


def own_kernel(place, *refs):
    ins, outs, rest = refs[:5], refs[5:9], refs[9:]
    held, made, in_sems, out_sems = rest[:5], rest[5:9], rest[9], rest[10]
    chip = place[1] * 2 + place[2]
    loads, stores = [], []
    for g in range(8):
        views = [ins[0].at[:, g]] + [ref.at[:, block_cols(g)] for ref in ins[1:]]
        loads.append([
            pltpu.make_async_copy(view, to.at[g], in_sems.at[n, g])
            for n, (view, to) in enumerate(zip(views, held))
        ])
        views = [outs[0].at[:, place[0], :, block_cols(g)]]
        views += [ref.at[:, block_cols(g)] for ref in outs[1:]]
        stores.append([
            pltpu.make_async_copy(of.at[g], view, out_sems.at[n, g])
            for n, (of, view) in enumerate(zip(made, views))
        ])
    for copies in loads:
        for copy in copies:
            copy.start()
    moved, before, merged, momentum, params = held
    full, new_params, new_momentum, new_error = made
    for g in range(8):
        for copy in loads[g]:
            copy.wait()
        for n, delta in enumerate(put_weights(moved.at[g], before.at[g], full.at[g], chip)):
            at = (g, slice(None), slice(n * 128, (n + 1) * 128))
            delta = delta.astype(F32)
            new_error[at] = merged[at] - delta
            step = 0.9 * momentum[at] + delta
            new_momentum[at] = step
            new_params[at] = params[at] - 0.7 * (delta + 0.9 * step)
        for copy in stores[g]:
            copy.start()
    for copies in stores:
        for copy in copies:
            copy.wait()


FULL_SHAPE = jax.ShapeDtypeStruct((8, 2, 32, 8192), BF16)
SMEM = pl.BlockSpec(memory_space=pltpu.SMEM)
ANYWHERE = pl.BlockSpec(memory_space=pl.ANY)


def own_rows(place, moved, before, merged, momentum, params):
    row_shape = jax.ShapeDtypeStruct((32, 8192), F32)
    rows = pltpu.VMEM((8, 32, 1024), F32)
    weights = pltpu.VMEM((8, 8, 32, 1024), BF16)
    return pl.pallas_call(
        own_kernel,
        in_specs=[SMEM] + [ANYWHERE] * 5,
        out_specs=[ANYWHERE] * 4,
        out_shape=[FULL_SHAPE, row_shape, row_shape, row_shape],
        scratch_shapes=[
            pltpu.VMEM((8, 8, 256, 128), BF16), pltpu.VMEM((8, 32, 1024), BF16), rows, rows, rows,
            weights, rows, rows, rows,
            pltpu.SemaphoreType.DMA((5, 8)),
            pltpu.SemaphoreType.DMA((4, 8)),
        ],
        compiler_params=pltpu.CompilerParams(vmem_limit_bytes=VMEM),
    )(place, moved.reshape(8, 8, 256, 128), before, merged, momentum, params)


def other_kernel(place, moved, before, _, full, held, held_before, made, sems, before_sems, out_sems):
    side, chip = 1 - place[0], place[1] * 2 + place[2]
    loads = [
        [
            pltpu.make_async_copy(moved.at[:, g], held.at[g], sems.at[g]),
            pltpu.make_async_copy(before.at[:, block_cols(g)], held_before.at[g], before_sems.at[g]),
        ]
        for g in range(8)
    ]
    stores = [
        pltpu.make_async_copy(made.at[g], full.at[:, side, :, block_cols(g)], out_sems.at[g])
        for g in range(8)
    ]
    for copies in loads:
        for copy in copies:
            copy.start()
    for g in range(8):
        for copy in loads[g]:
            copy.wait()
        put_weights(held.at[g], held_before.at[g], made.at[g], chip)
        stores[g].start()
    for copy in stores:
        copy.wait()


def other_rows(place, moved, before, full):
    return pl.pallas_call(
        other_kernel,
        in_specs=[SMEM] + [ANYWHERE] * 3,
        out_specs=ANYWHERE,
        out_shape=FULL_SHAPE,
        input_output_aliases={3: 0},
        scratch_shapes=[
            pltpu.VMEM((8, 8, 256, 128), BF16),
            pltpu.VMEM((8, 32, 1024), BF16),
            pltpu.VMEM((8, 8, 32, 1024), BF16),
            pltpu.SemaphoreType.DMA((8,)),
            pltpu.SemaphoreType.DMA((8,)),
            pltpu.SemaphoreType.DMA((8,)),
        ],
        compiler_params=pltpu.CompilerParams(vmem_limit_bytes=VMEM),
    )(place, moved.reshape(8, 8, 256, 128), before, full)


def middle_kernel(place, blocks, q_own, q_other, mean, out):
    total = blocks[0].astype(F32)
    for n in range(1, 8):
        total = total + blocks[n].astype(F32)
    low = (total * 0.125).astype(BF16)
    mean[...] = low
    low = jnp.concatenate([low[n] for n in range(8)], 1)
    for flag, q_ref in ((1, q_own), (0, q_other)):

        @pl.when(place[3] == flag)
        def _():
            value = dot_nn(low, q_ref[...]).astype(BF16)
            for n in range(8):
                out[n] = value


def middle(place, blocks, q_own, q_other):
    vmem = pl.BlockSpec(memory_space=pltpu.VMEM)
    return pl.pallas_call(
        middle_kernel,
        in_specs=[SMEM] + [vmem] * 3,
        out_specs=[vmem] * 2,
        out_shape=[
            pltpu.VMEM((8, 32, 128), BF16),
            jax.ShapeDtypeStruct((8, 32, 256), BF16),
        ],
    )(place, blocks, q_own, q_other)


def gather_kernel(terms, mean, before, out):
    total = terms[0].astype(F32)
    for n in range(1, 8):
        total = total + terms[n].astype(F32)
    total = total.astype(BF16)
    for n in range(8):
        out[n, 0] = total[:, :128]
        out[n, 1] = total[:, 128:]
        out[n, 2] = mean[n]
        out[n, 3] = before[n]


def gathered(terms, mean, before):
    vmem = pl.BlockSpec(memory_space=pltpu.VMEM)
    return pl.pallas_call(
        gather_kernel,
        in_specs=[vmem] * 3,
        out_specs=vmem,
        out_shape=jax.ShapeDtypeStruct((8, 4, 32, 128), BF16),
    )(terms, mean, before)


def merge_kernel(left, back, right, far, up, down, error, merged, blocks):
    for n in range(64):
        at = slice((n % 32) * 128, (n % 32 + 1) * 128)
        if n < 32:
            value = left[:, at] + back[:, at].astype(F32)
        else:
            value = right[:, at]
            for ref in (far, up, down):
                value = value + ref[:, at].astype(F32)
        value = value + error[:, n * 128 : (n + 1) * 128]
        merged[:, n * 128 : (n + 1) * 128] = value
        blocks[n % 8, n // 8] = value.astype(BF16)


def merge(left, back, right, moved, error):
    vmem = pl.BlockSpec(memory_space=pltpu.VMEM)
    return pl.pallas_call(
        merge_kernel,
        in_specs=[vmem] * 7,
        out_specs=[vmem] * 2,
        out_shape=[
            jax.ShapeDtypeStruct((32, 8192), F32),
            jax.ShapeDtypeStruct((8, 8, 32, 128), BF16),
        ],
    )(left, back, right, *moved, error)


def swap_cores(value):
    return lax.ppermute(value, "core", SWAP)


def along_z(value, step):
    return lax.ppermute(value, "z", [(at, (at + step) % 4) for at in range(4)])


def ring_order(ring, z):
    ring = jnp.stack([ring[0], ring[3], ring[2], ring[1]])
    return lax.dynamic_slice_in_dim(jnp.concatenate([ring, ring]), (4 - z) % 4, 4, 0)


def block_at(place, k, j, side):
    return lax.rem(place[1] + k, 4) * 4 + lax.rem(place[2] + j, 2) * 2 + lax.rem(place[0] + side, 2)


BLOCKS = [(k, j) for k in range(4) for j in range(2)]


def block_copies(place, parts, out, sems, side, half):
    return [
        pltpu.make_async_copy(
            parts.at[block_at(place, k, j, side), :, pl.ds(half * WIDE, WIDE)],
            out.at[k, j],
            sems.at[k, j],
        )
        for k, j in BLOCKS
    ]


def theirs_kernel(half, place, parts, out, sems):
    copies = block_copies(place, parts, out, sems, 1, half)
    for copy in copies:
        copy.start()
    for copy in copies:
        copy.wait()


def theirs(place, parts, half):
    return pl.pallas_call(
        functools.partial(theirs_kernel, half),
        in_specs=[
            pl.BlockSpec(memory_space=pltpu.SMEM),
            pl.BlockSpec(memory_space=pl.ANY),
        ],
        out_specs=pl.BlockSpec(memory_space=pltpu.VMEM),
        out_shape=pltpu.VMEM((4, 2, 32, WIDE), BF16),
        scratch_shapes=[pltpu.SemaphoreType.DMA((4, 2))],
    )(place, parts)


def add(left, right):
    return (left.astype(F32) + right.astype(F32)).astype(BF16)


def pair_sums(half, place, parts, received, ours, theirs, sems, in_sems):
    copies = list(zip(
        block_copies(place, parts, ours, sems, 0, half),
        [pltpu.make_async_copy(received.at[k, j], theirs.at[k, j], in_sems.at[k, j]) for k, j in BLOCKS],
    ))
    for own, other in copies:
        own.start()
        other.start()
    for (k, j), (own, other) in zip(BLOCKS, copies):
        own.wait()
        other.wait()
        yield k, j, add(ours[k, j], theirs[k, j])


def right_kernel(place, parts, received, keep, send, *scratch):
    for k, j, total in pair_sums(1, place, parts, received, *scratch):
        (send if j else keep)[k] = total


def left_kernel(place, parts, received, piece, keep, up, far, down, *scratch):
    outs = (keep, up, far, down)
    for out in outs[1:]:
        out[:, WIDE:] = piece[...]
    for k, j, total in pair_sums(0, place, parts, received, *scratch):
        outs[k][32 * j : 32 * j + 32, :WIDE] = total


def pair_call(kernel, shapes, place, parts, received, *rest):
    vmem = pl.BlockSpec(memory_space=pltpu.VMEM)
    anywhere = pl.BlockSpec(memory_space=pl.ANY)
    return pl.pallas_call(
        kernel,
        in_specs=[pl.BlockSpec(memory_space=pltpu.SMEM), anywhere, anywhere] + [vmem] * len(rest),
        out_specs=[vmem] * len(shapes),
        out_shape=[pltpu.VMEM(shape, BF16) for shape in shapes],
        scratch_shapes=[pltpu.VMEM((4, 2, 32, WIDE), BF16)] * 2 + [pltpu.SemaphoreType.DMA((4, 2))] * 2,
    )(place, parts, received, *rest)


def turn_kernel(left, up, far, down, piece, keep, back):
    def total(rows):
        value = left[rows, :].astype(F32)
        for ref in (up, far, down):
            value = value + ref[rows, :WIDE].astype(F32)
        return value

    keep[...] = total(slice(0, 32))
    back[:, :WIDE] = total(slice(32, 64)).astype(BF16)
    for k, ref in enumerate((piece, up, far, down)):
        at = 0 if k == 0 else WIDE
        for j in range(2):
            back[:, WIDE + k * 1024 + j * 512 : WIDE + k * 1024 + (j + 1) * 512] = ref[
                32 * j : 32 * j + 32, at : at + 512
            ]


def turn(left, up, far, down, piece):
    vmem = pl.BlockSpec(memory_space=pltpu.VMEM)
    return pl.pallas_call(
        turn_kernel,
        in_specs=[vmem] * 5,
        out_specs=[vmem] * 2,
        out_shape=[pltpu.VMEM((32, WIDE), F32), pltpu.VMEM((32, 2 * WIDE), BF16)],
    )(left, up, far, down, piece)


def summed_rows(partials, error, piece, place, z, yhi):
    parts = partials.reshape(16, 32, 8192)
    left_out, parts_later = lax.optimization_barrier((theirs(place, parts, 0), parts))
    left_in, right_in = swap_cores(left_out), swap_cores(theirs(place, parts_later, 1))
    shapes = [(64, WIDE)] + [(64, WIDE + 512)] * 3
    left, up, far, down = pair_call(left_kernel, shapes, place, parts, left_in, piece)
    right_in, left = lax.optimization_barrier((right_in, left))
    right, across = pair_call(right_kernel, [(4, 32, WIDE)] * 2, place, parts, right_in)
    across = lax.ppermute(across, "yhi", SWAP)
    far, up, down = along_z(far, 2), along_z(up, 1), along_z(down, 3)
    sums = [right[k].astype(F32) + across[k].astype(F32) for k in range(4)]
    moved = [along_z(sums[k].astype(BF16), k) for k in (2, 1, 3)]
    left, sent = turn(left, up, far, down, piece)
    back = lax.ppermute(sent, "yhi", SWAP)
    merged, blocks = merge(left, back, sums[0], moved, error)
    ours, others = (
        ring_order([value[:, WIDE + k * 1024 : WIDE + (k + 1) * 1024] for k in range(4)], z)
        for value in (sent, back)
    )
    pieces = jnp.where(yhi == 0, jnp.stack([ours, others], 1), jnp.stack([others, ours], 1))
    return merged, blocks, pieces.reshape(8, 32, 4, 256)


def on_device(partials, error_buf, momentum, params, start_q):
    core, z, yhi = (lax.axis_index(name) for name in ("core", "z", "yhi"))
    isl = lax.axis_index(ISLAND)
    place = jnp.stack([core, z, yhi, isl // 4 == core]).astype(jnp.int32)

    own_q = lax.dynamic_slice(start_q, ((isl % 4) * 128, 0), (128, 256)).astype(BF16)
    piece = jnp.concatenate([own_q[:64], own_q[64:]], 1)
    merged, blocks, pieces = summed_rows(partials[0, 0], error_buf[0], piece, place, z, yhi)
    q_own = jnp.stack([pieces[:, :, n] for n in (0, 2, 1, 3)], 1).reshape(1024, 256)
    q_other = swap_cores(q_own)

    before = (params - (0.7 * 0.9 * 0.9) * momentum).astype(BF16)
    before = lax.optimization_barrier(before)
    before_other = swap_cores(before)
    columns = lax.dynamic_index_in_dim(before.reshape(32, 8, 8, 128), isl, 2, False)
    columns = columns.transpose(1, 0, 2)

    blocks = lax.all_to_all(blocks, ISLAND, 0, 0, tiled=True)
    mean, terms = middle(place, blocks, q_own, q_other)
    terms = lax.all_to_all(terms, ISLAND, 0, 0, tiled=True)

    own = lax.all_to_all(gathered(terms, mean, columns), ZY, 0, 0, tiled=True)
    own = own.transpose(1, 0, 2, 3).reshape(4, 256, 128)
    own, before_other = lax.optimization_barrier((own, before_other))
    other = swap_cores(own)

    moved_own = lax.all_to_all(factors(own, other), CHIPS, 0, 0, tiled=True)
    moved_other = swap_cores(moved_own)
    params_full, new_params, new_momentum, new_error = own_rows(
        place, moved_own, before, merged, momentum, params
    )
    params_full = other_rows(place, moved_other, before_other, params_full)
    return (params_full.reshape(512, 8192), new_params, new_momentum, new_error[None])


def solution(mesh):
    fine = Mesh(mesh.devices.reshape(4, 2, 4, 2, 2), ("x", "ylo", "z", "yhi", "core"))
    in_specs = (
        P(ISLAND, SHARD, None, None),
        P(ISLAND, SHARD, None),
        P(SHARD, None),
        P(SHARD, None),
        P(SHARD, None),
    )
    out_specs = (P(), P(SHARD, None), P(SHARD, None), P(ISLAND, SHARD, None))
    return jax.shard_map(
        on_device, mesh=fine, in_specs=in_specs, out_specs=out_specs, check_vma=False
    )
```

```python
import functools

import jax
import jax.numpy as jnp
from jax import lax
from jax.experimental import pallas as pl
from jax.experimental.pallas import tpu as pltpu
from jax.sharding import Mesh
from jax.sharding import PartitionSpec as P

NS_ITERS = 5
F32 = jnp.float32
BF16 = jnp.bfloat16
ISLAND = ("x", "ylo")
ZY = ("z", "yhi")
SHARD = ("z", "yhi", "core")
SWAP = [(0, 1), (1, 0)]
CHIPS = ("x", "ylo", "z", "yhi")
WIDE = 4096
VMEM = 60 * 1024 * 1024


def dot_nn(left, right):
    return jnp.dot(left, right, preferred_element_type=F32)


def dot_tn(left, right):
    return lax.dot_general(left, right, (((0,), (0,)), ((), ())), preferred_element_type=F32)


def dot_nt(left, right):
    return lax.dot_general(left, right, (((1,), (1,)), ((), ())), preferred_element_type=F32)


def updated(before, delta):
    return (before.astype(F32) - (0.7 * 1.9) * delta.astype(F32)).astype(BF16)


def factor_kernel(own_ref, other_ref, out):
    def left_factor(ref):
        return jnp.concatenate([ref[0], ref[1]], 1).astype(F32)

    own, other = left_factor(own_ref), left_factor(other_ref)
    scale = lax.rsqrt(jnp.sum(own * own) + jnp.sum(other * other) + 1e-06)
    own, other = own * scale, other * scale
    for _ in range(NS_ITERS):
        low_own, low_other = own.astype(BF16), other.astype(BF16)
        gram_mat = (dot_tn(low_own, low_own) + dot_tn(low_other, low_other)).astype(BF16)
        own = 1.5 * own - 0.5 * dot_nn(low_own, gram_mat)
        other = 1.5 * other - 0.5 * dot_nn(low_other, gram_mat)
    low_own, low_other = own.astype(BF16), other.astype(BF16)
    qnew = dot_tn(own_ref[2], low_own) + dot_tn(other_ref[2], low_other)
    delta = dot_nt(low_own, qnew.astype(BF16)).astype(BF16)
    weights = updated(own_ref[3], delta)
    delta = delta.reshape(8, 32, 128)

    @pl.loop(0, 8)
    def _(island):
        for chip in range(8):
            out[island * 8 + chip] = weights
            out[island * 8 + chip, chip * 32 : chip * 32 + 32] = delta[chip]


def factors(own, other):
    vmem = pl.BlockSpec(memory_space=pltpu.VMEM)
    return pl.pallas_call(
        factor_kernel,
        in_specs=[vmem, vmem],
        out_specs=vmem,
        out_shape=jax.ShapeDtypeStruct((64, 256, 128), BF16),
        compiler_params=pltpu.CompilerParams(vmem_limit_bytes=32 * 1024 * 1024),
    )(own, other)


def block_cols(g):
    return pl.ds(g * 1024, 1024)


def put_weights(moved, before, full, chip):
    at = pl.ds(pl.multiple_of(chip * 32, 32), 32)
    deltas = []
    for n in range(8):
        cols = slice(n * 128, (n + 1) * 128)
        full[:, :, cols] = moved[n].reshape(8, 32, 128)
        deltas.append(moved[n, at, :])
        full[pl.ds(chip, 1), :, cols] = updated(before[:, cols], deltas[n])[None]
    return deltas


def own_kernel(place, *refs):
    ins, outs, rest = refs[:5], refs[5:9], refs[9:]
    held, made, in_sems, out_sems = rest[:5], rest[5:9], rest[9], rest[10]
    chip = place[1] * 2 + place[2]
    loads, stores = [], []
    for g in range(8):
        views = [ins[0].at[:, g]] + [ref.at[:, block_cols(g)] for ref in ins[1:]]
        loads.append([
            pltpu.make_async_copy(view, to.at[g], in_sems.at[n, g])
            for n, (view, to) in enumerate(zip(views, held))
        ])
        views = [outs[0].at[:, place[0], :, block_cols(g)]]
        views += [ref.at[:, block_cols(g)] for ref in outs[1:]]
        stores.append([
            pltpu.make_async_copy(of.at[g], view, out_sems.at[n, g])
            for n, (of, view) in enumerate(zip(made, views))
        ])
    for copies in loads:
        for copy in copies:
            copy.start()
    moved, before, merged, momentum, params = held
    full, new_params, new_momentum, new_error = made
    for g in range(8):
        for copy in loads[g]:
            copy.wait()
        for n, delta in enumerate(put_weights(moved.at[g], before.at[g], full.at[g], chip)):
            at = (g, slice(None), slice(n * 128, (n + 1) * 128))
            delta = delta.astype(F32)
            new_error[at] = merged[at] - delta
            step = 0.9 * momentum[at] + delta
            new_momentum[at] = step
            new_params[at] = params[at] - 0.7 * (delta + 0.9 * step)
        for copy in stores[g]:
            copy.start()
    for copies in stores:
        for copy in copies:
            copy.wait()


FULL_SHAPE = jax.ShapeDtypeStruct((8, 2, 32, 8192), BF16)
SMEM = pl.BlockSpec(memory_space=pltpu.SMEM)
ANYWHERE = pl.BlockSpec(memory_space=pl.ANY)


def own_rows(place, moved, before, merged, momentum, params):
    row_shape = jax.ShapeDtypeStruct((32, 8192), F32)
    rows = pltpu.VMEM((8, 32, 1024), F32)
    weights = pltpu.VMEM((8, 8, 32, 1024), BF16)
    return pl.pallas_call(
        own_kernel,
        in_specs=[SMEM] + [ANYWHERE] * 5,
        out_specs=[ANYWHERE] * 4,
        out_shape=[FULL_SHAPE, row_shape, row_shape, row_shape],
        scratch_shapes=[
            pltpu.VMEM((8, 8, 256, 128), BF16), pltpu.VMEM((8, 32, 1024), BF16), rows, rows, rows,
            weights, rows, rows, rows,
            pltpu.SemaphoreType.DMA((5, 8)),
            pltpu.SemaphoreType.DMA((4, 8)),
        ],
        compiler_params=pltpu.CompilerParams(vmem_limit_bytes=VMEM),
    )(place, moved.reshape(8, 8, 256, 128), before, merged, momentum, params)


def other_kernel(place, moved, before, _, full, held, held_before, made, sems, before_sems, out_sems):
    side, chip = 1 - place[0], place[1] * 2 + place[2]
    loads = [
        [
            pltpu.make_async_copy(moved.at[:, g], held.at[g], sems.at[g]),
            pltpu.make_async_copy(before.at[:, block_cols(g)], held_before.at[g], before_sems.at[g]),
        ]
        for g in range(8)
    ]
    stores = [
        pltpu.make_async_copy(made.at[g], full.at[:, side, :, block_cols(g)], out_sems.at[g])
        for g in range(8)
    ]
    for copies in loads:
        for copy in copies:
            copy.start()
    for g in range(8):
        for copy in loads[g]:
            copy.wait()
        put_weights(held.at[g], held_before.at[g], made.at[g], chip)
        stores[g].start()
    for copy in stores:
        copy.wait()


def other_rows(place, moved, before, full):
    return pl.pallas_call(
        other_kernel,
        in_specs=[SMEM] + [ANYWHERE] * 3,
        out_specs=ANYWHERE,
        out_shape=FULL_SHAPE,
        input_output_aliases={3: 0},
        scratch_shapes=[
            pltpu.VMEM((8, 8, 256, 128), BF16),
            pltpu.VMEM((8, 32, 1024), BF16),
            pltpu.VMEM((8, 8, 32, 1024), BF16),
            pltpu.SemaphoreType.DMA((8,)),
            pltpu.SemaphoreType.DMA((8,)),
            pltpu.SemaphoreType.DMA((8,)),
        ],
        compiler_params=pltpu.CompilerParams(vmem_limit_bytes=VMEM),
    )(place, moved.reshape(8, 8, 256, 128), before, full)


def middle_kernel(place, blocks, q_own, q_other, mean, out):
    total = blocks[0].astype(F32)
    for n in range(1, 8):
        total = total + blocks[n].astype(F32)
    low = (total * 0.125).astype(BF16)
    mean[...] = low
    low = jnp.concatenate([low[n] for n in range(8)], 1)
    for flag, q_ref in ((1, q_own), (0, q_other)):

        @pl.when(place[3] == flag)
        def _():
            value = dot_nn(low, q_ref[...]).astype(BF16)
            for n in range(8):
                out[n] = value


def middle(place, blocks, q_own, q_other):
    vmem = pl.BlockSpec(memory_space=pltpu.VMEM)
    return pl.pallas_call(
        middle_kernel,
        in_specs=[SMEM] + [vmem] * 3,
        out_specs=[vmem] * 2,
        out_shape=[
            pltpu.VMEM((8, 32, 128), BF16),
            jax.ShapeDtypeStruct((8, 32, 256), BF16),
        ],
    )(place, blocks, q_own, q_other)


def gather_kernel(terms, mean, before, out):
    total = terms[0].astype(F32)
    for n in range(1, 8):
        total = total + terms[n].astype(F32)
    total = total.astype(BF16)
    for n in range(8):
        out[n, 0] = total[:, :128]
        out[n, 1] = total[:, 128:]
        out[n, 2] = mean[n]
        out[n, 3] = before[n]


def gathered(terms, mean, before):
    vmem = pl.BlockSpec(memory_space=pltpu.VMEM)
    return pl.pallas_call(
        gather_kernel,
        in_specs=[vmem] * 3,
        out_specs=vmem,
        out_shape=jax.ShapeDtypeStruct((8, 4, 32, 128), BF16),
    )(terms, mean, before)


def merge_kernel(left, back, right, far, up, down, error, merged, blocks):
    for n in range(64):
        at = slice((n % 32) * 128, (n % 32 + 1) * 128)
        if n < 32:
            value = left[:, at] + back[:, at].astype(F32)
        else:
            value = right[:, at]
            for ref in (far, up, down):
                value = value + ref[:, at].astype(F32)
        value = value + error[:, n * 128 : (n + 1) * 128]
        merged[:, n * 128 : (n + 1) * 128] = value
        blocks[n % 8, n // 8] = value.astype(BF16)


def merge(left, back, right, moved, error):
    vmem = pl.BlockSpec(memory_space=pltpu.VMEM)
    return pl.pallas_call(
        merge_kernel,
        in_specs=[vmem] * 7,
        out_specs=[vmem] * 2,
        out_shape=[
            jax.ShapeDtypeStruct((32, 8192), F32),
            jax.ShapeDtypeStruct((8, 8, 32, 128), BF16),
        ],
    )(left, back, right, *moved, error)


def swap_cores(value):
    return lax.ppermute(value, "core", SWAP)


def along_z(value, step):
    return lax.ppermute(value, "z", [(at, (at + step) % 4) for at in range(4)])


def ring_order(ring, z):
    ring = jnp.stack([ring[0], ring[3], ring[2], ring[1]])
    return lax.dynamic_slice_in_dim(jnp.concatenate([ring, ring]), (4 - z) % 4, 4, 0)


def block_at(place, k, j, side):
    return lax.rem(place[1] + k, 4) * 4 + lax.rem(place[2] + j, 2) * 2 + lax.rem(place[0] + side, 2)


BLOCKS = [(k, j) for k in range(4) for j in range(2)]


def block_copies(place, parts, out, sems, side, half):
    return [
        pltpu.make_async_copy(
            parts.at[block_at(place, k, j, side), :, pl.ds(half * WIDE, WIDE)],
            out.at[k, j],
            sems.at[k, j],
        )
        for k, j in BLOCKS
    ]


def theirs_kernel(half, place, parts, out, held, in_sems, out_sems):
    loads = block_copies(place, parts, held, in_sems, 1, half)
    stores = [pltpu.make_async_copy(held.at[k, j], out.at[k, j], out_sems.at[k, j]) for k, j in BLOCKS]
    for load in loads:
        load.start()
    for load, store in zip(loads, stores):
        load.wait()
        store.start()
    for store in stores:
        store.wait()


def theirs(place, parts, half):
    shape = (4, 2, 32, WIDE)
    return pl.pallas_call(
        functools.partial(theirs_kernel, half),
        in_specs=[SMEM, ANYWHERE],
        out_specs=ANYWHERE,
        out_shape=jax.ShapeDtypeStruct(shape, BF16),
        scratch_shapes=[pltpu.VMEM(shape, BF16)] + [pltpu.SemaphoreType.DMA((4, 2))] * 2,
    )(place, parts)


def add(left, right):
    return (left.astype(F32) + right.astype(F32)).astype(BF16)


def pair_sums(half, place, parts, received, ours, theirs, sems, in_sems):
    copies = list(zip(
        block_copies(place, parts, ours, sems, 0, half),
        [pltpu.make_async_copy(received.at[k, j], theirs.at[k, j], in_sems.at[k, j]) for k, j in BLOCKS],
    ))
    for own, other in copies:
        own.start()
        other.start()
    for (k, j), (own, other) in zip(BLOCKS, copies):
        own.wait()
        other.wait()
        yield k, j, add(ours[k, j], theirs[k, j])


def right_kernel(place, parts, received, keep, send, made, out_sems, *scratch):
    stores = []
    for k, j, total in pair_sums(1, place, parts, received, *scratch):
        made[k, j] = total
        stores.append(pltpu.make_async_copy(made.at[k, j], (send if j else keep).at[k], out_sems.at[k, j]))
        stores[-1].start()
    for store in stores:
        store.wait()


def left_kernel(place, parts, received, piece, keep, up, far, down, made, out_sems, *scratch):
    outs, stores = (keep, up, far, down), []
    for k, j, total in pair_sums(0, place, parts, received, *scratch):
        made[k, 32 * j : 32 * j + 32, :WIDE] = total
        if j == 0:
            made[k, :, WIDE:] = piece[...]
            continue
        view = made.at[k] if k else made.at[k, :, pl.ds(0, WIDE)]
        stores.append(pltpu.make_async_copy(view, outs[k], out_sems.at[k, 0]))
        stores[-1].start()
    for store in stores:
        store.wait()


def pair_call(kernel, shapes, made, place, parts, received, *rest):
    vmem = pl.BlockSpec(memory_space=pltpu.VMEM)
    return pl.pallas_call(
        kernel,
        in_specs=[SMEM, ANYWHERE, ANYWHERE] + [vmem] * len(rest),
        out_specs=[ANYWHERE] * len(shapes),
        out_shape=[jax.ShapeDtypeStruct(shape, BF16) for shape in shapes],
        scratch_shapes=[pltpu.VMEM(made, BF16), pltpu.SemaphoreType.DMA((4, 2))]
        + [pltpu.VMEM((4, 2, 32, WIDE), BF16)] * 2
        + [pltpu.SemaphoreType.DMA((4, 2))] * 2,
        compiler_params=pltpu.CompilerParams(vmem_limit_bytes=VMEM),
    )(place, parts, received, *rest)


def turn_kernel(left, up, far, down, piece, keep, back):
    def total(rows):
        value = left[rows, :].astype(F32)
        for ref in (up, far, down):
            value = value + ref[rows, :WIDE].astype(F32)
        return value

    keep[...] = total(slice(0, 32))
    back[:, :WIDE] = total(slice(32, 64)).astype(BF16)
    for k, ref in enumerate((piece, up, far, down)):
        at = 0 if k == 0 else WIDE
        for j in range(2):
            back[:, WIDE + k * 1024 + j * 512 : WIDE + k * 1024 + (j + 1) * 512] = ref[
                32 * j : 32 * j + 32, at : at + 512
            ]


def turn(left, up, far, down, piece):
    vmem = pl.BlockSpec(memory_space=pltpu.VMEM)
    return pl.pallas_call(
        turn_kernel,
        in_specs=[vmem] * 5,
        out_specs=[vmem] * 2,
        out_shape=[pltpu.VMEM((32, WIDE), F32), pltpu.VMEM((32, 2 * WIDE), BF16)],
    )(left, up, far, down, piece)


def summed_rows(partials, error, piece, place, z, yhi):
    parts = partials.reshape(16, 32, 8192)
    left_out, parts_later = lax.optimization_barrier((theirs(place, parts, 0), parts))
    left_in, right_in = swap_cores(left_out), swap_cores(theirs(place, parts_later, 1))
    shapes = [(64, WIDE)] + [(64, WIDE + 512)] * 3
    left, up, far, down = pair_call(
        left_kernel, shapes, (4, 64, WIDE + 512), place, parts, left_in, piece
    )
    right_in, left = lax.optimization_barrier((right_in, left))
    right, across = pair_call(
        right_kernel, [(4, 32, WIDE)] * 2, (4, 2, 32, WIDE), place, parts, right_in
    )
    across = lax.ppermute(across, "yhi", SWAP)
    far, up, down = along_z(far, 2), along_z(up, 1), along_z(down, 3)
    sums = [right[k].astype(F32) + across[k].astype(F32) for k in range(4)]
    moved = [along_z(sums[k].astype(BF16), k) for k in (2, 1, 3)]
    left, sent = turn(left, up, far, down, piece)
    back = lax.ppermute(sent, "yhi", SWAP)
    merged, blocks = merge(left, back, sums[0], moved, error)
    ours, others = (
        ring_order([value[:, WIDE + k * 1024 : WIDE + (k + 1) * 1024] for k in range(4)], z)
        for value in (sent, back)
    )
    pieces = jnp.where(yhi == 0, jnp.stack([ours, others], 1), jnp.stack([others, ours], 1))
    return merged, blocks, pieces.reshape(8, 32, 4, 256)


def on_device(partials, error_buf, momentum, params, start_q):
    core, z, yhi = (lax.axis_index(name) for name in ("core", "z", "yhi"))
    isl = lax.axis_index(ISLAND)
    place = jnp.stack([core, z, yhi, isl // 4 == core]).astype(jnp.int32)

    own_q = lax.dynamic_slice(start_q, ((isl % 4) * 128, 0), (128, 256)).astype(BF16)
    piece = jnp.concatenate([own_q[:64], own_q[64:]], 1)
    merged, blocks, pieces = summed_rows(partials[0, 0], error_buf[0], piece, place, z, yhi)
    q_own = jnp.stack([pieces[:, :, n] for n in (0, 2, 1, 3)], 1).reshape(1024, 256)
    q_other = swap_cores(q_own)

    before = (params - (0.7 * 0.9 * 0.9) * momentum).astype(BF16)
    before = lax.optimization_barrier(before)
    before_other = swap_cores(before)
    columns = lax.dynamic_index_in_dim(before.reshape(32, 8, 8, 128), isl, 2, False)
    columns = columns.transpose(1, 0, 2)

    blocks = lax.all_to_all(blocks, ISLAND, 0, 0, tiled=True)
    mean, terms = middle(place, blocks, q_own, q_other)
    terms = lax.all_to_all(terms, ISLAND, 0, 0, tiled=True)

    own = lax.all_to_all(gathered(terms, mean, columns), ZY, 0, 0, tiled=True)
    own = own.transpose(1, 0, 2, 3).reshape(4, 256, 128)
    own, before_other = lax.optimization_barrier((own, before_other))
    other = swap_cores(own)

    moved_own = lax.all_to_all(factors(own, other), CHIPS, 0, 0, tiled=True)
    moved_other = swap_cores(moved_own)
    params_full, new_params, new_momentum, new_error = own_rows(
        place, moved_own, before, merged, momentum, params
    )
    params_full = other_rows(place, moved_other, before_other, params_full)
    return (params_full.reshape(512, 8192), new_params, new_momentum, new_error[None])


def solution(mesh):
    fine = Mesh(mesh.devices.reshape(4, 2, 4, 2, 2), ("x", "ylo", "z", "yhi", "core"))
    in_specs = (
        P(ISLAND, SHARD, None, None),
        P(ISLAND, SHARD, None),
        P(SHARD, None),
        P(SHARD, None),
        P(SHARD, None),
    )
    out_specs = (P(), P(SHARD, None), P(SHARD, None), P(ISLAND, SHARD, None))
    return jax.shard_map(
        on_device, mesh=fine, in_specs=in_specs, out_specs=out_specs, check_vma=False
    )
```

```python
import functools

import jax
import jax.numpy as jnp
from jax import lax
from jax.experimental import pallas as pl
from jax.experimental.pallas import tpu as pltpu
from jax.sharding import Mesh
from jax.sharding import PartitionSpec as P

NS_ITERS = 5
F32 = jnp.float32
BF16 = jnp.bfloat16
ISLAND = ("x", "ylo")
ZY = ("z", "yhi")
SHARD = ("z", "yhi", "core")
SWAP = [(0, 1), (1, 0)]
CHIPS = ("x", "ylo", "z", "yhi")
WIDE = 4096
VMEM = 60 * 1024 * 1024


def dot_nn(left, right):
    return jnp.dot(left, right, preferred_element_type=F32)


def dot_tn(left, right):
    return lax.dot_general(left, right, (((0,), (0,)), ((), ())), preferred_element_type=F32)


def dot_nt(left, right):
    return lax.dot_general(left, right, (((1,), (1,)), ((), ())), preferred_element_type=F32)


def updated(before, delta):
    return (before.astype(F32) - (0.7 * 1.9) * delta.astype(F32)).astype(BF16)


def factor_kernel(own_ref, other_ref, out):
    def left_factor(ref):
        return jnp.concatenate([ref[0], ref[1]], 1).astype(F32)

    own, other = left_factor(own_ref), left_factor(other_ref)
    scale = lax.rsqrt(jnp.sum(own * own) + jnp.sum(other * other) + 1e-06)
    own, other = own * scale, other * scale
    for _ in range(NS_ITERS):
        low_own, low_other = own.astype(BF16), other.astype(BF16)
        gram_mat = (dot_tn(low_own, low_own) + dot_tn(low_other, low_other)).astype(BF16)
        own = 1.5 * own - 0.5 * dot_nn(low_own, gram_mat)
        other = 1.5 * other - 0.5 * dot_nn(low_other, gram_mat)
    low_own, low_other = own.astype(BF16), other.astype(BF16)
    qnew = dot_tn(own_ref[2], low_own) + dot_tn(other_ref[2], low_other)
    delta = dot_nt(low_own, qnew.astype(BF16)).astype(BF16)
    weights = updated(own_ref[3], delta)
    delta = delta.reshape(8, 32, 128)

    @pl.loop(0, 8)
    def _(island):
        for chip in range(8):
            out[island * 8 + chip] = weights
            out[island * 8 + chip, chip * 32 : chip * 32 + 32] = delta[chip]


def factors(own, other):
    vmem = pl.BlockSpec(memory_space=pltpu.VMEM)
    return pl.pallas_call(
        factor_kernel,
        in_specs=[vmem, vmem],
        out_specs=vmem,
        out_shape=jax.ShapeDtypeStruct((64, 256, 128), BF16),
        compiler_params=pltpu.CompilerParams(vmem_limit_bytes=32 * 1024 * 1024),
    )(own, other)


def block_cols(g):
    return pl.ds(g * 1024, 1024)


def put_weights(moved, before, full, chip):
    at = pl.ds(pl.multiple_of(chip * 32, 32), 32)
    deltas = []
    for n in range(8):
        cols = slice(n * 128, (n + 1) * 128)
        full[:, :, cols] = moved[n].reshape(8, 32, 128)
        deltas.append(moved[n, at, :])
        full[pl.ds(chip, 1), :, cols] = updated(before[:, cols], deltas[n])[None]
    return deltas


def own_kernel(place, *refs):
    ins, outs, rest = refs[:5], refs[5:9], refs[9:]
    held, made, in_sems, out_sems = rest[:5], rest[5:9], rest[9], rest[10]
    chip = place[1] * 2 + place[2]
    loads, stores = [], []
    for g in range(8):
        views = [ins[0].at[:, g]] + [ref.at[:, block_cols(g)] for ref in ins[1:]]
        loads.append([
            pltpu.make_async_copy(view, to.at[g], in_sems.at[n, g])
            for n, (view, to) in enumerate(zip(views, held))
        ])
        views = [outs[0].at[:, place[0], :, block_cols(g)]]
        views += [ref.at[:, block_cols(g)] for ref in outs[1:]]
        stores.append([
            pltpu.make_async_copy(of.at[g], view, out_sems.at[n, g])
            for n, (of, view) in enumerate(zip(made, views))
        ])
    for copies in loads:
        for copy in copies:
            copy.start()
    moved, before, merged, momentum, params = held
    full, new_params, new_momentum, new_error = made
    for g in range(8):
        for copy in loads[g]:
            copy.wait()
        for n, delta in enumerate(put_weights(moved.at[g], before.at[g], full.at[g], chip)):
            at = (g, slice(None), slice(n * 128, (n + 1) * 128))
            delta = delta.astype(F32)
            new_error[at] = merged[at] - delta
            step = 0.9 * momentum[at] + delta
            new_momentum[at] = step
            new_params[at] = params[at] - 0.7 * (delta + 0.9 * step)
        for copy in stores[g]:
            copy.start()
    for copies in stores:
        for copy in copies:
            copy.wait()


FULL_SHAPE = jax.ShapeDtypeStruct((8, 2, 32, 8192), BF16)
SMEM = pl.BlockSpec(memory_space=pltpu.SMEM)
ANYWHERE = pl.BlockSpec(memory_space=pl.ANY)


def own_rows(place, moved, before, merged, momentum, params):
    row_shape = jax.ShapeDtypeStruct((32, 8192), F32)
    rows = pltpu.VMEM((8, 32, 1024), F32)
    weights = pltpu.VMEM((8, 8, 32, 1024), BF16)
    return pl.pallas_call(
        own_kernel,
        in_specs=[SMEM] + [ANYWHERE] * 5,
        out_specs=[ANYWHERE] * 4,
        out_shape=[FULL_SHAPE, row_shape, row_shape, row_shape],
        scratch_shapes=[
            pltpu.VMEM((8, 8, 256, 128), BF16), pltpu.VMEM((8, 32, 1024), BF16), rows, rows, rows,
            weights, rows, rows, rows,
            pltpu.SemaphoreType.DMA((5, 8)),
            pltpu.SemaphoreType.DMA((4, 8)),
        ],
        compiler_params=pltpu.CompilerParams(vmem_limit_bytes=VMEM),
    )(place, moved.reshape(8, 8, 256, 128), before, merged, momentum, params)


def other_kernel(place, moved, before, _, full, held, held_before, made, sems, before_sems, out_sems):
    side, chip = 1 - place[0], place[1] * 2 + place[2]
    loads = [
        [
            pltpu.make_async_copy(moved.at[:, g], held.at[g], sems.at[g]),
            pltpu.make_async_copy(before.at[:, block_cols(g)], held_before.at[g], before_sems.at[g]),
        ]
        for g in range(8)
    ]
    stores = [
        pltpu.make_async_copy(made.at[g], full.at[:, side, :, block_cols(g)], out_sems.at[g])
        for g in range(8)
    ]
    for copies in loads:
        for copy in copies:
            copy.start()
    for g in range(8):
        for copy in loads[g]:
            copy.wait()
        put_weights(held.at[g], held_before.at[g], made.at[g], chip)
        stores[g].start()
    for copy in stores:
        copy.wait()


def other_rows(place, moved, before, full):
    return pl.pallas_call(
        other_kernel,
        in_specs=[SMEM] + [ANYWHERE] * 3,
        out_specs=ANYWHERE,
        out_shape=FULL_SHAPE,
        input_output_aliases={3: 0},
        scratch_shapes=[
            pltpu.VMEM((8, 8, 256, 128), BF16),
            pltpu.VMEM((8, 32, 1024), BF16),
            pltpu.VMEM((8, 8, 32, 1024), BF16),
            pltpu.SemaphoreType.DMA((8,)),
            pltpu.SemaphoreType.DMA((8,)),
            pltpu.SemaphoreType.DMA((8,)),
        ],
        compiler_params=pltpu.CompilerParams(vmem_limit_bytes=VMEM),
    )(place, moved.reshape(8, 8, 256, 128), before, full)


def middle_kernel(place, blocks, q_own, q_other, mean, out):
    total = blocks[0].astype(F32)
    for n in range(1, 8):
        total = total + blocks[n].astype(F32)
    low = (total * 0.125).astype(BF16)
    mean[...] = low
    low = jnp.concatenate([low[n] for n in range(8)], 1)
    for flag, q_ref in ((1, q_own), (0, q_other)):

        @pl.when(place[3] == flag)
        def _():
            value = dot_nn(low, q_ref[...]).astype(BF16)
            for n in range(8):
                out[n] = value


def middle(place, blocks, q_own, q_other):
    vmem = pl.BlockSpec(memory_space=pltpu.VMEM)
    return pl.pallas_call(
        middle_kernel,
        in_specs=[SMEM] + [vmem] * 3,
        out_specs=[vmem] * 2,
        out_shape=[
            pltpu.VMEM((8, 32, 128), BF16),
            jax.ShapeDtypeStruct((8, 32, 256), BF16),
        ],
    )(place, blocks, q_own, q_other)


def gather_kernel(terms, mean, before, out):
    total = terms[0].astype(F32)
    for n in range(1, 8):
        total = total + terms[n].astype(F32)
    total = total.astype(BF16)
    for n in range(8):
        out[n, 0] = total[:, :128]
        out[n, 1] = total[:, 128:]
        out[n, 2] = mean[n]
        out[n, 3] = before[n]


def gathered(terms, mean, before):
    vmem = pl.BlockSpec(memory_space=pltpu.VMEM)
    return pl.pallas_call(
        gather_kernel,
        in_specs=[vmem] * 3,
        out_specs=vmem,
        out_shape=jax.ShapeDtypeStruct((8, 4, 32, 128), BF16),
    )(terms, mean, before)


def merge_kernel(left, back, right, far, up, down, error, merged, blocks):
    for n in range(64):
        at = slice((n % 32) * 128, (n % 32 + 1) * 128)
        if n < 32:
            value = left[:, at] + back[:, at].astype(F32)
        else:
            value = right[:, at]
            for ref in (far, up, down):
                value = value + ref[:, at].astype(F32)
        value = value + error[:, n * 128 : (n + 1) * 128]
        merged[:, n * 128 : (n + 1) * 128] = value
        blocks[n % 8, n // 8] = value.astype(BF16)


def merge(left, back, right, moved, error):
    vmem = pl.BlockSpec(memory_space=pltpu.VMEM)
    return pl.pallas_call(
        merge_kernel,
        in_specs=[vmem] * 7,
        out_specs=[vmem] * 2,
        out_shape=[
            jax.ShapeDtypeStruct((32, 8192), F32),
            jax.ShapeDtypeStruct((8, 8, 32, 128), BF16),
        ],
    )(left, back, right, *moved, error)


def swap_cores(value):
    return lax.ppermute(value, "core", SWAP)


def along_z(value, step):
    return lax.ppermute(value, "z", [(at, (at + step) % 4) for at in range(4)])


def ring_order(ring, z):
    ring = jnp.stack([ring[0], ring[3], ring[2], ring[1]])
    return lax.dynamic_slice_in_dim(jnp.concatenate([ring, ring]), (4 - z) % 4, 4, 0)


def block_at(place, k, j, side):
    return lax.rem(place[1] + k, 4) * 4 + lax.rem(place[2] + j, 2) * 2 + lax.rem(place[0] + side, 2)


BLOCKS = [(k, j) for k in range(4) for j in range(2)]


def block_copies(place, parts, out, sems, side, half):
    return [
        pltpu.make_async_copy(
            parts.at[block_at(place, k, j, side), :, pl.ds(half * WIDE, WIDE)],
            out.at[k, j],
            sems.at[k, j],
        )
        for k, j in BLOCKS
    ]


def theirs_kernel(half, parts, out, held, in_sems, out_sems):
    place = [lax.axis_index(name) for name in ("core", "z", "yhi")]
    loads = block_copies(place, parts, held, in_sems, 1, half)
    stores = [pltpu.make_async_copy(held.at[k, j], out.at[k, j], out_sems.at[k, j]) for k, j in BLOCKS]
    for load in loads:
        load.start()
    for load, store in zip(loads, stores):
        load.wait()
        store.start()
    for store in stores:
        store.wait()


def theirs(parts, half):
    shape = (4, 2, 32, WIDE)
    return pl.pallas_call(
        functools.partial(theirs_kernel, half),
        in_specs=[ANYWHERE],
        out_specs=ANYWHERE,
        out_shape=jax.ShapeDtypeStruct(shape, BF16),
        scratch_shapes=[pltpu.VMEM(shape, BF16)] + [pltpu.SemaphoreType.DMA((4, 2))] * 2,
    )(parts)


def add(left, right):
    return (left.astype(F32) + right.astype(F32)).astype(BF16)


def pair_sums(half, place, parts, received, ours, theirs, sems, in_sems):
    copies = list(zip(
        block_copies(place, parts, ours, sems, 0, half),
        [pltpu.make_async_copy(received.at[k, j], theirs.at[k, j], in_sems.at[k, j]) for k, j in BLOCKS],
    ))
    for own, other in copies:
        own.start()
        other.start()
    for (k, j), (own, other) in zip(BLOCKS, copies):
        own.wait()
        other.wait()
        yield k, j, add(ours[k, j], theirs[k, j])


def right_kernel(place, parts, received, keep, send, made, out_sems, *scratch):
    stores = []
    for k, j, total in pair_sums(1, place, parts, received, *scratch):
        made[k, j] = total
        stores.append(pltpu.make_async_copy(made.at[k, j], (send if j else keep).at[k], out_sems.at[k, j]))
        stores[-1].start()
    for store in stores:
        store.wait()


def left_kernel(place, parts, received, piece, keep, up, far, down, made, out_sems, *scratch):
    outs, stores = (keep, up, far, down), []
    for k, j, total in pair_sums(0, place, parts, received, *scratch):
        made[k, 32 * j : 32 * j + 32, :WIDE] = total
        if j == 0:
            made[k, :, WIDE:] = piece[...]
            continue
        view = made.at[k] if k else made.at[k, :, pl.ds(0, WIDE)]
        stores.append(pltpu.make_async_copy(view, outs[k], out_sems.at[k, 0]))
        stores[-1].start()
    for store in stores:
        store.wait()


def pair_call(kernel, shapes, made, place, parts, received, *rest):
    vmem = pl.BlockSpec(memory_space=pltpu.VMEM)
    return pl.pallas_call(
        kernel,
        in_specs=[SMEM, ANYWHERE, ANYWHERE] + [vmem] * len(rest),
        out_specs=[ANYWHERE] * len(shapes),
        out_shape=[jax.ShapeDtypeStruct(shape, BF16) for shape in shapes],
        scratch_shapes=[pltpu.VMEM(made, BF16), pltpu.SemaphoreType.DMA((4, 2))]
        + [pltpu.VMEM((4, 2, 32, WIDE), BF16)] * 2
        + [pltpu.SemaphoreType.DMA((4, 2))] * 2,
        compiler_params=pltpu.CompilerParams(vmem_limit_bytes=VMEM),
    )(place, parts, received, *rest)


def turn_kernel(left, up, far, down, piece, keep, back):
    def total(rows):
        value = left[rows, :].astype(F32)
        for ref in (up, far, down):
            value = value + ref[rows, :WIDE].astype(F32)
        return value

    keep[...] = total(slice(0, 32))
    back[:, :WIDE] = total(slice(32, 64)).astype(BF16)
    for k, ref in enumerate((piece, up, far, down)):
        at = 0 if k == 0 else WIDE
        for j in range(2):
            back[:, WIDE + k * 1024 + j * 512 : WIDE + k * 1024 + (j + 1) * 512] = ref[
                32 * j : 32 * j + 32, at : at + 512
            ]


def turn(left, up, far, down, piece):
    vmem = pl.BlockSpec(memory_space=pltpu.VMEM)
    return pl.pallas_call(
        turn_kernel,
        in_specs=[vmem] * 5,
        out_specs=[vmem] * 2,
        out_shape=[pltpu.VMEM((32, WIDE), F32), pltpu.VMEM((32, 2 * WIDE), BF16)],
    )(left, up, far, down, piece)


def summed_rows(partials, error, piece, place, z, yhi):
    parts = partials.reshape(16, 32, 8192)
    left_out, parts_later = lax.optimization_barrier((theirs(parts, 0), parts))
    left_in, right_in = swap_cores(left_out), swap_cores(theirs(parts_later, 1))
    shapes = [(64, WIDE)] + [(64, WIDE + 512)] * 3
    left, up, far, down = pair_call(
        left_kernel, shapes, (4, 64, WIDE + 512), place, parts, left_in, piece
    )
    right_in, left = lax.optimization_barrier((right_in, left))
    right, across = pair_call(
        right_kernel, [(4, 32, WIDE)] * 2, (4, 2, 32, WIDE), place, parts, right_in
    )
    across = lax.ppermute(across, "yhi", SWAP)
    far, up, down = along_z(far, 2), along_z(up, 1), along_z(down, 3)
    sums = [right[k].astype(F32) + across[k].astype(F32) for k in range(4)]
    moved = [along_z(sums[k].astype(BF16), k) for k in (2, 1, 3)]
    left, sent = turn(left, up, far, down, piece)
    back = lax.ppermute(sent, "yhi", SWAP)
    merged, blocks = merge(left, back, sums[0], moved, error)
    ours, others = (
        ring_order([value[:, WIDE + k * 1024 : WIDE + (k + 1) * 1024] for k in range(4)], z)
        for value in (sent, back)
    )
    pieces = jnp.where(yhi == 0, jnp.stack([ours, others], 1), jnp.stack([others, ours], 1))
    return merged, blocks, pieces.reshape(8, 32, 4, 256)


def on_device(partials, error_buf, momentum, params, start_q):
    core, z, yhi = (lax.axis_index(name) for name in ("core", "z", "yhi"))
    isl = lax.axis_index(ISLAND)
    place = jnp.stack([core, z, yhi, isl // 4 == core]).astype(jnp.int32)

    own_q = lax.dynamic_slice(start_q, ((isl % 4) * 128, 0), (128, 256)).astype(BF16)
    piece = jnp.concatenate([own_q[:64], own_q[64:]], 1)
    merged, blocks, pieces = summed_rows(partials[0, 0], error_buf[0], piece, place, z, yhi)
    q_own = jnp.stack([pieces[:, :, n] for n in (0, 2, 1, 3)], 1).reshape(1024, 256)
    q_other = swap_cores(q_own)

    before = (params - (0.7 * 0.9 * 0.9) * momentum).astype(BF16)
    before = lax.optimization_barrier(before)
    before_other = swap_cores(before)
    columns = lax.dynamic_index_in_dim(before.reshape(32, 8, 8, 128), isl, 2, False)
    columns = columns.transpose(1, 0, 2)

    blocks = lax.all_to_all(blocks, ISLAND, 0, 0, tiled=True)
    mean, terms = middle(place, blocks, q_own, q_other)
    terms = lax.all_to_all(terms, ISLAND, 0, 0, tiled=True)

    own = lax.all_to_all(gathered(terms, mean, columns), ZY, 0, 0, tiled=True)
    own = own.transpose(1, 0, 2, 3).reshape(4, 256, 128)
    own, before_other = lax.optimization_barrier((own, before_other))
    other = swap_cores(own)

    moved_own = lax.all_to_all(factors(own, other), CHIPS, 0, 0, tiled=True)
    moved_other = swap_cores(moved_own)
    params_full, new_params, new_momentum, new_error = own_rows(
        place, moved_own, before, merged, momentum, params
    )
    params_full = other_rows(place, moved_other, before_other, params_full)
    return (params_full.reshape(512, 8192), new_params, new_momentum, new_error[None])


def solution(mesh):
    fine = Mesh(mesh.devices.reshape(4, 2, 4, 2, 2), ("x", "ylo", "z", "yhi", "core"))
    in_specs = (
        P(ISLAND, SHARD, None, None),
        P(ISLAND, SHARD, None),
        P(SHARD, None),
        P(SHARD, None),
        P(SHARD, None),
    )
    out_specs = (P(), P(SHARD, None), P(SHARD, None), P(ISLAND, SHARD, None))
    return jax.shard_map(
        on_device, mesh=fine, in_specs=in_specs, out_specs=out_specs, check_vma=False
    )
```

```python
import functools

import jax
import jax.numpy as jnp
from jax import lax
from jax.experimental import pallas as pl
from jax.experimental.pallas import tpu as pltpu
from jax.sharding import Mesh
from jax.sharding import PartitionSpec as P

NS_ITERS = 5
F32 = jnp.float32
BF16 = jnp.bfloat16
ISLAND = ("x", "ylo")
ZY = ("z", "yhi")
SHARD = ("z", "yhi", "core")
SWAP = [(0, 1), (1, 0)]
CHIPS = ("x", "ylo", "z", "yhi")
WIDE = 4096
VMEM = 60 * 1024 * 1024


def dot_nn(left, right):
    return jnp.dot(left, right, preferred_element_type=F32)


def dot_tn(left, right):
    return lax.dot_general(left, right, (((0,), (0,)), ((), ())), preferred_element_type=F32)


def dot_nt(left, right):
    return lax.dot_general(left, right, (((1,), (1,)), ((), ())), preferred_element_type=F32)


def updated(before, delta):
    return (before.astype(F32) - (0.7 * 1.9) * delta.astype(F32)).astype(BF16)


def factor_kernel(own_ref, other_ref, out):
    def left_factor(ref):
        return jnp.concatenate([ref[0], ref[1]], 1).astype(F32)

    own, other = left_factor(own_ref), left_factor(other_ref)
    scale = lax.rsqrt(jnp.sum(own * own) + jnp.sum(other * other) + 1e-06)
    own, other = own * scale, other * scale
    for _ in range(NS_ITERS):
        low_own, low_other = own.astype(BF16), other.astype(BF16)
        gram_mat = (dot_tn(low_own, low_own) + dot_tn(low_other, low_other)).astype(BF16)
        own = 1.5 * own - 0.5 * dot_nn(low_own, gram_mat)
        other = 1.5 * other - 0.5 * dot_nn(low_other, gram_mat)
    low_own, low_other = own.astype(BF16), other.astype(BF16)
    qnew = dot_tn(own_ref[2], low_own) + dot_tn(other_ref[2], low_other)
    delta = dot_nt(low_own, qnew.astype(BF16)).astype(BF16)
    weights = updated(own_ref[3], delta)
    delta = delta.reshape(8, 32, 128)

    @pl.loop(0, 8)
    def _(island):
        for chip in range(8):
            out[island * 8 + chip] = weights
            out[island * 8 + chip, chip * 32 : chip * 32 + 32] = delta[chip]


def factors(own, other):
    vmem = pl.BlockSpec(memory_space=pltpu.VMEM)
    return pl.pallas_call(
        factor_kernel,
        in_specs=[vmem, vmem],
        out_specs=vmem,
        out_shape=jax.ShapeDtypeStruct((64, 256, 128), BF16),
        compiler_params=pltpu.CompilerParams(vmem_limit_bytes=32 * 1024 * 1024),
    )(own, other)


def block_cols(g):
    return pl.ds(g * 1024, 1024)


def put_weights(moved, before, full, chip):
    at = pl.ds(pl.multiple_of(chip * 32, 32), 32)
    deltas = []
    for n in range(8):
        cols = slice(n * 128, (n + 1) * 128)
        full[:, :, cols] = moved[n].reshape(8, 32, 128)
        deltas.append(moved[n, at, :])
        full[pl.ds(chip, 1), :, cols] = updated(before[:, cols], deltas[n])[None]
    return deltas


def own_kernel(place, *refs):
    ins, outs, rest = refs[:5], refs[5:9], refs[9:]
    held, made, in_sems, out_sems = rest[:5], rest[5:9], rest[9], rest[10]
    chip = place[1] * 2 + place[2]
    loads, stores = [], []
    for g in range(8):
        views = [ins[0].at[:, g]] + [ref.at[:, block_cols(g)] for ref in ins[1:]]
        loads.append([
            pltpu.make_async_copy(view, to.at[g], in_sems.at[n, g])
            for n, (view, to) in enumerate(zip(views, held))
        ])
        views = [outs[0].at[:, place[0], :, block_cols(g)]]
        views += [ref.at[:, block_cols(g)] for ref in outs[1:]]
        stores.append([
            pltpu.make_async_copy(of.at[g], view, out_sems.at[n, g])
            for n, (of, view) in enumerate(zip(made, views))
        ])
    for copies in loads:
        for copy in copies:
            copy.start()
    moved, before, merged, momentum, params = held
    full, new_params, new_momentum, new_error = made
    for g in range(8):
        for copy in loads[g]:
            copy.wait()
        for n, delta in enumerate(put_weights(moved.at[g], before.at[g], full.at[g], chip)):
            at = (g, slice(None), slice(n * 128, (n + 1) * 128))
            delta = delta.astype(F32)
            new_error[at] = merged[at] - delta
            step = 0.9 * momentum[at] + delta
            new_momentum[at] = step
            new_params[at] = params[at] - 0.7 * (delta + 0.9 * step)
        for copy in stores[g]:
            copy.start()
    for copies in stores:
        for copy in copies:
            copy.wait()


FULL_SHAPE = jax.ShapeDtypeStruct((8, 2, 32, 8192), BF16)
SMEM = pl.BlockSpec(memory_space=pltpu.SMEM)
ANYWHERE = pl.BlockSpec(memory_space=pl.ANY)


def own_rows(place, moved, before, merged, momentum, params):
    row_shape = jax.ShapeDtypeStruct((32, 8192), F32)
    rows = pltpu.VMEM((8, 32, 1024), F32)
    weights = pltpu.VMEM((8, 8, 32, 1024), BF16)
    return pl.pallas_call(
        own_kernel,
        in_specs=[SMEM] + [ANYWHERE] * 5,
        out_specs=[ANYWHERE] * 4,
        out_shape=[FULL_SHAPE, row_shape, row_shape, row_shape],
        scratch_shapes=[
            pltpu.VMEM((8, 8, 256, 128), BF16), pltpu.VMEM((8, 32, 1024), BF16), rows, rows, rows,
            weights, rows, rows, rows,
            pltpu.SemaphoreType.DMA((5, 8)),
            pltpu.SemaphoreType.DMA((4, 8)),
        ],
        compiler_params=pltpu.CompilerParams(vmem_limit_bytes=VMEM),
    )(place, moved.reshape(8, 8, 256, 128), before, merged, momentum, params)


def other_kernel(place, moved, before, _, full, held, held_before, made, sems, before_sems, out_sems):
    side, chip = 1 - place[0], place[1] * 2 + place[2]
    loads = [
        [
            pltpu.make_async_copy(moved.at[:, g], held.at[g], sems.at[g]),
            pltpu.make_async_copy(before.at[:, block_cols(g)], held_before.at[g], before_sems.at[g]),
        ]
        for g in range(8)
    ]
    stores = [
        pltpu.make_async_copy(made.at[g], full.at[:, side, :, block_cols(g)], out_sems.at[g])
        for g in range(8)
    ]
    for copies in loads:
        for copy in copies:
            copy.start()
    for g in range(8):
        for copy in loads[g]:
            copy.wait()
        put_weights(held.at[g], held_before.at[g], made.at[g], chip)
        stores[g].start()
    for copy in stores:
        copy.wait()


def other_rows(place, moved, before, full):
    return pl.pallas_call(
        other_kernel,
        in_specs=[SMEM] + [ANYWHERE] * 3,
        out_specs=ANYWHERE,
        out_shape=FULL_SHAPE,
        input_output_aliases={3: 0},
        scratch_shapes=[
            pltpu.VMEM((8, 8, 256, 128), BF16),
            pltpu.VMEM((8, 32, 1024), BF16),
            pltpu.VMEM((8, 8, 32, 1024), BF16),
            pltpu.SemaphoreType.DMA((8,)),
            pltpu.SemaphoreType.DMA((8,)),
            pltpu.SemaphoreType.DMA((8,)),
        ],
        compiler_params=pltpu.CompilerParams(vmem_limit_bytes=VMEM),
    )(place, moved.reshape(8, 8, 256, 128), before, full)


def middle_kernel(place, blocks, q_own, q_other, mean, out):
    total = blocks[0].astype(F32)
    for n in range(1, 8):
        total = total + blocks[n].astype(F32)
    low = (total * 0.125).astype(BF16)
    mean[...] = low
    low = jnp.concatenate([low[n] for n in range(8)], 1)
    for flag, q_ref in ((1, q_own), (0, q_other)):

        @pl.when(place[3] == flag)
        def _():
            value = dot_nn(low, q_ref[...]).astype(BF16)
            for n in range(8):
                out[n] = value


def middle(place, blocks, q_own, q_other):
    vmem = pl.BlockSpec(memory_space=pltpu.VMEM)
    return pl.pallas_call(
        middle_kernel,
        in_specs=[SMEM] + [vmem] * 3,
        out_specs=[vmem] * 2,
        out_shape=[
            pltpu.VMEM((8, 32, 128), BF16),
            jax.ShapeDtypeStruct((8, 32, 256), BF16),
        ],
    )(place, blocks, q_own, q_other)


def gather_kernel(terms, mean, before, out):
    total = terms[0].astype(F32)
    for n in range(1, 8):
        total = total + terms[n].astype(F32)
    total = total.astype(BF16)
    for n in range(8):
        out[n, 0] = total[:, :128]
        out[n, 1] = total[:, 128:]
        out[n, 2] = mean[n]
        out[n, 3] = before[n]


def gathered(terms, mean, before):
    vmem = pl.BlockSpec(memory_space=pltpu.VMEM)
    return pl.pallas_call(
        gather_kernel,
        in_specs=[vmem] * 3,
        out_specs=vmem,
        out_shape=jax.ShapeDtypeStruct((8, 4, 32, 128), BF16),
    )(terms, mean, before)


def merge_kernel(left, back, right, far, up, down, error, merged, blocks):
    for n in range(64):
        at = slice((n % 32) * 128, (n % 32 + 1) * 128)
        if n < 32:
            value = left[:, at] + back[:, at].astype(F32)
        else:
            value = right[:, at]
            for ref in (far, up, down):
                value = value + ref[:, at].astype(F32)
        value = value + error[:, n * 128 : (n + 1) * 128]
        merged[:, n * 128 : (n + 1) * 128] = value
        blocks[n % 8, n // 8] = value.astype(BF16)


def merge(left, back, right, moved, error):
    vmem = pl.BlockSpec(memory_space=pltpu.VMEM)
    return pl.pallas_call(
        merge_kernel,
        in_specs=[vmem] * 7,
        out_specs=[vmem] * 2,
        out_shape=[
            jax.ShapeDtypeStruct((32, 8192), F32),
            jax.ShapeDtypeStruct((8, 8, 32, 128), BF16),
        ],
    )(left, back, right, *moved, error)


def swap_cores(value):
    return lax.ppermute(value, "core", SWAP)


def along_z(value, step):
    return lax.ppermute(value, "z", [(at, (at + step) % 4) for at in range(4)])


def ring_order(ring, z):
    ring = jnp.stack([ring[0], ring[3], ring[2], ring[1]])
    return lax.dynamic_slice_in_dim(jnp.concatenate([ring, ring]), (4 - z) % 4, 4, 0)


def block_at(place, k, j, side):
    return lax.rem(place[1] + k, 4) * 4 + lax.rem(place[2] + j, 2) * 2 + lax.rem(place[0] + side, 2)


BLOCKS = [(k, j) for k in range(4) for j in range(2)]


def block_copies(place, parts, out, sems, side, half):
    return [
        pltpu.make_async_copy(
            parts.at[block_at(place, k, j, side), :, pl.ds(half * WIDE, WIDE)],
            out.at[k, j],
            sems.at[k, j],
        )
        for k, j in BLOCKS
    ]


def theirs_kernel(half, parts, out, held, in_sems, out_sems):
    place = [lax.axis_index(name) for name in ("core", "z", "yhi")]
    loads = block_copies(place, parts, held, in_sems, 1, half)
    stores = [pltpu.make_async_copy(held.at[k, j], out.at[k, j], out_sems.at[k, j]) for k, j in BLOCKS]
    for load in loads:
        load.start()
    for load, store in zip(loads, stores):
        load.wait()
        store.start()
    for store in stores:
        store.wait()


def theirs(parts, half):
    shape = (4, 2, 32, WIDE)
    return pl.pallas_call(
        functools.partial(theirs_kernel, half),
        in_specs=[ANYWHERE],
        out_specs=ANYWHERE,
        out_shape=jax.ShapeDtypeStruct(shape, BF16),
        scratch_shapes=[pltpu.VMEM(shape, BF16)] + [pltpu.SemaphoreType.DMA((4, 2))] * 2,
    )(parts)


def add(left, right):
    return (left.astype(F32) + right.astype(F32)).astype(BF16)


def pair_sums(half, place, parts, received, ours, theirs, sems, in_sems):
    copies = list(zip(
        block_copies(place, parts, ours, sems, 0, half),
        [pltpu.make_async_copy(received.at[k, j], theirs.at[k, j], in_sems.at[k, j]) for k, j in BLOCKS],
    ))
    for own, other in copies:
        own.start()
        other.start()
    for (k, j), (own, other) in zip(BLOCKS, copies):
        own.wait()
        other.wait()
        yield k, j, add(ours[k, j], theirs[k, j])


def right_kernel(place, parts, received, keep, send, made, out_sems, *scratch):
    stores = []
    for k, j, total in pair_sums(1, place, parts, received, *scratch):
        made[k, j] = total
        stores.append(pltpu.make_async_copy(made.at[k, j], (send if j else keep).at[k], out_sems.at[k, j]))
        stores[-1].start()
    for store in stores:
        store.wait()


def left_kernel(place, parts, received, piece, keep, up, far, down, made, out_sems, *scratch):
    outs, stores = (keep, up, far, down), []
    for k, j, total in pair_sums(0, place, parts, received, *scratch):
        made[k, 32 * j : 32 * j + 32, :WIDE] = total
        if j == 0:
            made[k, :, WIDE:] = piece[...]
            continue
        view = made.at[k] if k else made.at[k, :, pl.ds(0, WIDE)]
        stores.append(pltpu.make_async_copy(view, outs[k], out_sems.at[k, 0]))
        stores[-1].start()
    for store in stores:
        store.wait()


def pair_call(kernel, shapes, made, place, parts, received, *rest):
    vmem = pl.BlockSpec(memory_space=pltpu.VMEM)
    def placed(*refs):
        kernel([lax.axis_index(name) for name in ("core", "z", "yhi")], *refs)

    return pl.pallas_call(
        placed,
        in_specs=[ANYWHERE, ANYWHERE] + [vmem] * len(rest),
        out_specs=[ANYWHERE] * len(shapes),
        out_shape=[jax.ShapeDtypeStruct(shape, BF16) for shape in shapes],
        scratch_shapes=[pltpu.VMEM(made, BF16), pltpu.SemaphoreType.DMA((4, 2))]
        + [pltpu.VMEM((4, 2, 32, WIDE), BF16)] * 2
        + [pltpu.SemaphoreType.DMA((4, 2))] * 2,
        compiler_params=pltpu.CompilerParams(vmem_limit_bytes=VMEM),
    )(parts, received, *rest)


def turn_kernel(left, up, far, down, piece, keep, back):
    def total(rows):
        value = left[rows, :].astype(F32)
        for ref in (up, far, down):
            value = value + ref[rows, :WIDE].astype(F32)
        return value

    keep[...] = total(slice(0, 32))
    back[:, :WIDE] = total(slice(32, 64)).astype(BF16)
    for k, ref in enumerate((piece, up, far, down)):
        at = 0 if k == 0 else WIDE
        for j in range(2):
            back[:, WIDE + k * 1024 + j * 512 : WIDE + k * 1024 + (j + 1) * 512] = ref[
                32 * j : 32 * j + 32, at : at + 512
            ]


def turn(left, up, far, down, piece):
    vmem = pl.BlockSpec(memory_space=pltpu.VMEM)
    return pl.pallas_call(
        turn_kernel,
        in_specs=[vmem] * 5,
        out_specs=[vmem] * 2,
        out_shape=[pltpu.VMEM((32, WIDE), F32), pltpu.VMEM((32, 2 * WIDE), BF16)],
    )(left, up, far, down, piece)


def summed_rows(partials, error, piece, place, z, yhi):
    parts = partials.reshape(16, 32, 8192)
    left_out, parts_later = lax.optimization_barrier((theirs(parts, 0), parts))
    left_in, right_in = swap_cores(left_out), swap_cores(theirs(parts_later, 1))
    shapes = [(64, WIDE)] + [(64, WIDE + 512)] * 3
    left, up, far, down = pair_call(
        left_kernel, shapes, (4, 64, WIDE + 512), place, parts, left_in, piece
    )
    right_in, left = lax.optimization_barrier((right_in, left))
    right, across = pair_call(
        right_kernel, [(4, 32, WIDE)] * 2, (4, 2, 32, WIDE), place, parts, right_in
    )
    across = lax.ppermute(across, "yhi", SWAP)
    far, up, down = along_z(far, 2), along_z(up, 1), along_z(down, 3)
    sums = [right[k].astype(F32) + across[k].astype(F32) for k in range(4)]
    moved = [along_z(sums[k].astype(BF16), k) for k in (2, 1, 3)]
    left, sent = turn(left, up, far, down, piece)
    back = lax.ppermute(sent, "yhi", SWAP)
    merged, blocks = merge(left, back, sums[0], moved, error)
    ours, others = (
        ring_order([value[:, WIDE + k * 1024 : WIDE + (k + 1) * 1024] for k in range(4)], z)
        for value in (sent, back)
    )
    pieces = jnp.where(yhi == 0, jnp.stack([ours, others], 1), jnp.stack([others, ours], 1))
    return merged, blocks, pieces.reshape(8, 32, 4, 256)


def on_device(partials, error_buf, momentum, params, start_q):
    core, z, yhi = (lax.axis_index(name) for name in ("core", "z", "yhi"))
    isl = lax.axis_index(ISLAND)
    place = jnp.stack([core, z, yhi, isl // 4 == core]).astype(jnp.int32)

    own_q = lax.dynamic_slice(start_q, ((isl % 4) * 128, 0), (128, 256)).astype(BF16)
    piece = jnp.concatenate([own_q[:64], own_q[64:]], 1)
    merged, blocks, pieces = summed_rows(partials[0, 0], error_buf[0], piece, place, z, yhi)
    q_own = jnp.stack([pieces[:, :, n] for n in (0, 2, 1, 3)], 1).reshape(1024, 256)
    q_other = swap_cores(q_own)

    before = (params - (0.7 * 0.9 * 0.9) * momentum).astype(BF16)
    before = lax.optimization_barrier(before)
    before_other = swap_cores(before)
    columns = lax.dynamic_index_in_dim(before.reshape(32, 8, 8, 128), isl, 2, False)
    columns = columns.transpose(1, 0, 2)

    blocks = lax.all_to_all(blocks, ISLAND, 0, 0, tiled=True)
    mean, terms = middle(place, blocks, q_own, q_other)
    terms = lax.all_to_all(terms, ISLAND, 0, 0, tiled=True)

    own = lax.all_to_all(gathered(terms, mean, columns), ZY, 0, 0, tiled=True)
    own = own.transpose(1, 0, 2, 3).reshape(4, 256, 128)
    own, before_other = lax.optimization_barrier((own, before_other))
    other = swap_cores(own)

    moved_own = lax.all_to_all(factors(own, other), CHIPS, 0, 0, tiled=True)
    moved_other = swap_cores(moved_own)
    params_full, new_params, new_momentum, new_error = own_rows(
        place, moved_own, before, merged, momentum, params
    )
    params_full = other_rows(place, moved_other, before_other, params_full)
    return (params_full.reshape(512, 8192), new_params, new_momentum, new_error[None])


def solution(mesh):
    fine = Mesh(mesh.devices.reshape(4, 2, 4, 2, 2), ("x", "ylo", "z", "yhi", "core"))
    in_specs = (
        P(ISLAND, SHARD, None, None),
        P(ISLAND, SHARD, None),
        P(SHARD, None),
        P(SHARD, None),
        P(SHARD, None),
    )
    out_specs = (P(), P(SHARD, None), P(SHARD, None), P(ISLAND, SHARD, None))
    return jax.shard_map(
        on_device, mesh=fine, in_specs=in_specs, out_specs=out_specs, check_vma=False
    )
```
